256 devices in a mesh: row: 64 (over z, y, core), col: 4 (over x).
Axes of the slice: x: 4, y: 4, z: 8, core: 2. Of those that a mesh axis runs over, the one named last changes fastest.
Arguments:
- panel_col: float32 [131072, 256], P('row', 'col'), may hold values from -6 to 6
- look_cols: float32 [131072, 2048], P('row', 'col'), may hold values from -6 to 6
- sketch_map: float32 [256, 131072], P(None, 'row'), may hold values from -0.015625 to 0.015625
- upper_inv: float32 [256, 256], replicated, may hold values from -0.09375 to 0.09375
- lower_inv: float32 [256, 256], replicated, may hold values from -0.375 to 0.375
- pivots: int32 [256], replicated, may hold values from 256 to 131071, as said below
Outputs:
- l_panel: float32 [131072, 256], P('row', 'col')
- updated: float32 [131072, 2048], P('row', 'col')
- sketch: float32 [256, 256], P(None, 'col')
The draws below stay inside these ranges and needn't reach their ends.
Inputs may be any that keep to these rules, and one draw needn't show every extreme that they name: `pivots`: distinct rows, none of them among the first 256.
All inputs are finite; a program needn't handle non-finite values.
Results may differ from the reference program's by a relative error of at most 0.000073.
Values sent between devices are 32-bit elements; how exact they have to be, the bound alone decides.
A program may use at most 64 MiB of HBM per device.

```python
import jax
import jax.numpy as jnp
from jax import lax

NB = 256
W = 2048
KS = 256
ROWS_DEV = 2048
M = 131072


def draw_pivots(key, part):
    dev_count = M // ROWS_DEV
    base = jax.random.fold_in(key, 7)
    key_order, key_hot, key_one = jax.random.split(base, 3)
    order = jax.random.permutation(key_order, M).astype(jnp.int32)
    row_ids = jnp.arange(M, dtype=jnp.int32)
    dev_of = row_ids // ROWS_DEV
    hot_dev = jax.random.randint(key_hot, (dev_count,), 0, 4) == 0
    hot_dev = hot_dev | (jnp.arange(dev_count) == jax.random.randint(key_one, (), 0, dev_count))
    score = order + M * hot_dev[dev_of].astype(jnp.int32)
    score = jnp.where(row_ids < NB, -1 - row_ids, score)
    return lax.top_k(score, NB)[1].astype(jnp.int32)


def shard_levels(stream_key, shape, cuts, least, largest):
    level, own = 1.0, jax.random.fold_in(stream_key, 6)
    for dim, blocks in cuts:
        draws = jnp.exp(jax.random.uniform(jax.random.fold_in(own, dim), (blocks,), jnp.float32, least / len(cuts), largest / len(cuts)))
        level = level * jnp.repeat(draws, shape[dim] // blocks).reshape([-1 if axis == dim else 1 for axis in range(len(shape))])
    return level


def centred(own_key, shape, spread, most, cuts=(), kind=jnp.bfloat16):
    drawn = spread * jax.random.normal(own_key, shape, jnp.float32)
    if cuts:
        drawn = drawn * shard_levels(own_key, shape, cuts, -0.22, 0.18)
    return jnp.clip(drawn, -most, most).astype(kind)


def setup_inputs(seed: int = 0) -> dict:
    key_of = jax.random.split(jax.random.key(seed), 7)
    panel_col = centred(key_of[0], (M, NB), 1.0, 6.0, ((0, 64), (1, 4)), jnp.float32)
    look_cols = centred(key_of[1], (M, W), 1.0, 6.0, ((0, 64), (1, 4)), jnp.float32)
    sketch_map = centred(key_of[2], (KS, M), M ** -0.5, 0.015625, ((1, 64),), jnp.float32)
    upper_inv = centred(key_of[3], (NB, NB), (16 * NB) ** -0.5, 0.09375, (), jnp.float32)
    lower_inv = centred(key_of[4], (NB, NB), NB ** -0.5, 0.375, (), jnp.float32)
    pivots = draw_pivots(jax.random.fold_in(key_of[6], 71), 0)
    return {"panel_col": panel_col, "look_cols": look_cols, "sketch_map": sketch_map, "upper_inv": upper_inv, "lower_inv": lower_inv, "pivots": pivots}


high_prec = lax.Precision.HIGHEST


def swap_rows(matrix, pivots):
    initial = matrix[:NB]
    picked = matrix[pivots]
    return matrix.at[:NB].set(picked).at[pivots].set(initial)


def reference(panel_col, look_cols, sketch_map, upper_inv, lower_inv, pivots):
    sketch = jnp.dot(sketch_map, panel_col, precision=high_prec, preferred_element_type=jnp.float32)
    swapped_panel = swap_rows(panel_col, pivots)
    swapped_look = swap_rows(look_cols, pivots)
    upper_tri = jnp.triu(upper_inv)
    lower_tri = jnp.tril(lower_inv, -1) + jnp.eye(NB, dtype=jnp.float32)
    factor = jnp.dot(swapped_panel, upper_tri, precision=high_prec, preferred_element_type=jnp.float32)
    is_top = (jnp.arange(M) < NB)[:, None]
    l_panel = jnp.where(is_top, swapped_panel, factor)
    u_rows = jnp.dot(lower_tri, swapped_look[:NB], precision=high_prec, preferred_element_type=jnp.float32)
    updated = swapped_look - jnp.dot(factor, u_rows, precision=high_prec, preferred_element_type=jnp.float32)
    updated = updated.at[:NB].set(u_rows)
    return l_panel, updated, sketch
```

```python
import jax
import jax.numpy as jnp
from jax import lax
from jax.experimental import pallas as pl
from jax.experimental.pallas import tpu as pltpu
from jax.sharding import PartitionSpec as P

MESH = pl.DeviceIdType.MESH
F32, BF16 = jnp.float32, jnp.bfloat16
NB = 256
CY, CZ = 4, 8

X_RING = 0
A_CORE = 6
A_Y = 10
A_Z = 13
A_GZ = 20
A_GY = 27
A_GC = 30
S_CORE = 34
S_Z = 35
S_Y = 42
S_GZ = 45
S_GC = 52
H_X = 53
H_Z = 56
H_Y = 63
H_GZ = 66
H_GY = 73
H_GC = 76
N_SEM = 77


def split(a):
    hi = a.astype(BF16)
    return hi, (a - hi.astype(F32)).astype(BF16)


def dot(a, b, dims=((1,), (0,))):
    return lax.dot_general(a, b, (dims, ((), ())), preferred_element_type=F32)


def dot3(a, b, dims=((1,), (0,))):
    (ah, al), (bh, bl) = a, b
    return dot(ah, bh, dims) + dot(al, bh, dims) + dot(ah, bl, dims)


def comm_kernel(
    piv_s, piv_v, panel, look, smap,
    piv, head, red, ph, plo,
    look_v, sm_v, gath, pick, cbuf, hsum, ybuf, zin, zbuf,
    spart, scbuf, ssum, szbuf, sybuf, deal,
    ld, ss, rs,
):
    r, x = lax.axis_index("row"), lax.axis_index("col")
    c = lax.rem(r, 2)
    y = lax.rem(lax.div(r, 2), CY)
    z = lax.div(r, 2 * CY)
    first = r * look.shape[0]
    root = r == 0

    def to_x(d):
        return (r, lax.rem(x + d + 4, 4))

    def to_y(d):
        return ((z * CY + lax.rem(y + d, CY)) * 2 + c, x)

    def to_z(d):
        return ((lax.rem(z + d, CZ) * CY + y) * 2 + c, x)

    sibling = ((z * CY + y) * 2 + 1 - c, x)

    pending = []

    def remote(src, dst, slot, device, recv_slot=None):
        return pltpu.make_async_remote_copy(
            src_ref=src, dst_ref=dst, send_sem=ss.at[slot],
            recv_sem=rs.at[slot if recv_slot is None else recv_slot],
            device_id=device, device_id_type=MESH,
        )

    def send(*args):
        copy = remote(*args)
        copy.start()
        pending.append(copy)
        return copy

    def rows8(i):
        return pl.ds(pl.multiple_of(i * 8, 8), 8)

    def rows64(i):
        return pl.ds(pl.multiple_of(i * 64, 64), 64)

    mine = pl.ds(pl.multiple_of(c * 256, 256), 256)
    other = pl.ds(pl.multiple_of((1 - c) * 256, 256), 256)
    half_cols = gath.shape[1] // 2
    halves = [pl.ds(0, half_cols), pl.ds(half_cols, half_cols)]
    own_block = rows64(x)

    load_look = pltpu.make_async_copy(look, look_v, ld.at[0])
    load_look.start()
    load_panel = pltpu.make_async_copy(panel, gath.at[own_block, :], ld.at[1])
    load_panel.start()
    load_map = pltpu.make_async_copy(smap, sm_v, ld.at[2])
    load_map.start()

    bar = pltpu.get_barrier_semaphore()
    partners = [to_x(d) for d in (1, 2, 3)] + [to_y(d) for d in range(1, CY)]
    partners += [to_z(d) for d in range(1, CZ)] + [sibling]
    for device in partners:
        pl.semaphore_signal(bar, inc=1, device_id=device, device_id_type=MESH)

    load_look.wait()

    def pick_rows(i, carry):
        for k in range(8):
            row = i * 8 + k
            local = piv_s[row] - first
            owned = (local >= 0) & (local < look_v.shape[0])
            at = jnp.where(owned, local, 0)
            pick[pl.ds(row, 1), :] = jnp.where(owned, look_v[pl.ds(at, 1), :], 0.0)
        return carry

    lax.fori_loop(0, NB // 8, pick_rows, 0)
    pl.semaphore_wait(bar, len(partners))

    a_core = []
    for d in (1, 2, 3, 0):
        block = rows64(lax.rem(y + d, CY))
        a_core.append((d, block, send(pick.at[block, other], cbuf.at[block, :], A_CORE + d, sibling)))

    right, left = to_x(1), to_x(-1)
    ring = [
        send(panel.at[:, halves[0]], gath.at[own_block, halves[0]], X_RING, right),
        send(panel.at[:, halves[1]], gath.at[own_block, halves[1]], X_RING + 2, left),
        send(panel.at[:, halves[1]], gath.at[own_block, halves[1]], X_RING + 1, right),
        send(panel.at[:, halves[0]], gath.at[own_block, halves[0]], X_RING + 3, left),
    ]

    @pl.when(root)
    def _():
        local = [pltpu.make_async_copy(panel.at[:, pl.ds(0, NB)], deal.at[x, :, pl.ds(512, NB)], ld.at[3])]
        for q in range(CY):
            local.append(
                pltpu.make_async_copy(look.at[pl.ds(64 * q, 64), :], deal.at[q, :, pl.ds(0, 512)], ld.at[4 + q])
            )
        for copy in local:
            copy.start()
        sends = []
        for d in (1, 2, 3):
            sends.append(
                remote(panel.at[:, pl.ds(0, NB)], deal.at[x, :, pl.ds(512, NB)], H_X + d - 1, to_x(d))
            )
            sends[-1].start()
        for copy in local:
            copy.wait()
        for copy in sends:
            copy.wait()

    a_y = []
    for d, block, copy in a_core:
        copy.wait_recv()
        hsum[block, :] = pick[block, mine] + cbuf[block, :]
        if d:
            a_y.append(send(hsum.at[block, :], ybuf.at[d - 1], A_Y + d - 1, to_y(d)))

    @pl.when(root)
    def _():
        for d in range(1, CZ):
            remote(deal.at[:, pl.ds(8 * d, 8), :], deal.at[:, pl.ds(8 * d, 8), :], H_Z + d - 1, to_z(d), H_Z).start()

    load_panel.wait()
    load_map.wait()
    spart[...] = jnp.zeros_like(spart)
    tile = 512

    def small(i, carry):
        cols = pl.ds(pl.multiple_of(i * tile, tile), tile)
        p = gath[own_block, cols]
        p1, p2 = split(p)
        p3 = (p - p1.astype(F32) - p2.astype(F32)).astype(BF16)
        mh, ml = split(sm_v[:, cols])
        nt = ((1,), (1,))
        both = dot(jnp.concatenate([p1, p2], 0), mh, nt)
        spart[0:64, :] += both[0:64] + both[64:128] + dot(p1, ml, nt)
        at = lax.broadcasted_iota(jnp.int32, (tile, NB), 0) + (first + i * tile)
        hot = jnp.where(at == piv_v[...], 1.0, 0.0).astype(BF16)
        three = dot(jnp.concatenate([p1, p2, p3], 0), hot)
        spart[64:128, :] += three[0:64] + three[64:128] + three[128:192]
        return carry

    lax.fori_loop(0, gath.shape[1] // tile, small, 0)
    s_core = send(spart.at[rows64(1 - c), :], scbuf, S_CORE, sibling)

    for copy in a_y:
        copy.wait_recv()
    zin[...] = hsum[rows64(y), :] + ybuf[0] + ybuf[1] + ybuf[2]
    a_z = [send(zin.at[rows8(lax.rem(z + d, CZ)), :], zbuf.at[d - 1], A_Z + d - 1, to_z(d)) for d in range(1, CZ)]

    my_head = head.at[y, rows8(z), :]

    @pl.when((y == 0) & (c == 0))
    def _():
        @pl.when(z > 0)
        def _():
            landed = deal.at[:, rows8(z), :]
            remote(landed, landed, H_Z, to_z(1)).wait_recv()

        for d in range(1, CY):
            remote(deal.at[d, rows8(z), :], head.at[d, rows8(z), :], H_Y + d - 1, to_y(d), H_Y).start()
        head[0, rows8(z), :] = deal[0, rows8(z), :]

    s_core.wait_recv()
    ssum[...] = spart[rows64(c), :] + scbuf[...]
    s_z = [send(ssum.at[rows8(lax.rem(z + d, CZ)), :], szbuf.at[d - 1], S_Z + d - 1, to_z(d)) for d in range(1, CZ)]

    @pl.when(c == 0)
    def _():
        @pl.when(y > 0)
        def _():
            remote(my_head, my_head, H_Y, to_y(1)).wait_recv()

        for d in range(1, CZ):
            remote(my_head, my_head, H_GZ + d - 1, to_z(d)).start()

    ring[0].wait_recv()
    block = gath.at[rows64(lax.rem(x + 3, 4)), halves[0]]
    ring.append(send(block, block, X_RING + 4, right))
    ring[1].wait_recv()
    block = gath.at[rows64(lax.rem(x + 1, 4)), halves[1]]
    ring.append(send(block, block, X_RING + 5, left))

    for copy in a_z:
        copy.wait_recv()
    at_mine = pl.ds(pl.multiple_of(y * 64 + z * 8, 8), 8)
    total = zin[rows8(z), :]
    for d in range(1, CZ):
        total = total + zbuf[d - 1]
    piv[at_mine, mine] = total
    chunk = piv.at[at_mine, mine]
    a_gz = [send(chunk, chunk, A_GZ + d - 1, to_z(d)) for d in range(1, CZ)]

    @pl.when(c == 0)
    def _():
        for d in range(1, CZ):
            remote(my_head, my_head, H_GZ + d - 1, to_z(d)).wait_recv()
        for d in range(1, CY):
            remote(head.at[y], head.at[y], H_GY + d - 1, to_y(d)).start()

    for copy in s_z:
        copy.wait_recv()
    total = ssum[rows8(z), :]
    for d in range(1, CZ):
        total = total + szbuf[d - 1]
    sybuf[y] = total
    s_y = [send(sybuf.at[y], sybuf.at[y], S_Y + d - 1, to_y(d)) for d in range(1, CY)]

    for copy in a_gz:
        copy.wait_recv()
    quarter = piv.at[rows64(y), mine]
    a_gy = [send(quarter, quarter, A_GY + d - 1, to_y(d)) for d in range(1, CY)]
    a_gc = [send(quarter, quarter, A_GC, sibling)]

    for copy in s_y:
        copy.wait_recv()
    at_small = pl.ds(pl.multiple_of(c * 64 + z * 8, 8), 8)
    red[at_small, :] = sybuf[0] + sybuf[1] + sybuf[2] + sybuf[3]
    s_gz = [send(red.at[at_small, :], red.at[at_small, :], S_GZ + d - 1, to_z(d)) for d in range(1, CZ)]

    @pl.when(c == 0)
    def _():
        for d in range(1, CY):
            remote(head.at[y], head.at[y], H_GY + d - 1, to_y(d)).wait_recv()
        remote(head, head, H_GC, sibling).start()

    for copy in ring[2:]:
        copy.wait_recv()

    def turn(i, carry):
        at = pl.ds(pl.multiple_of(i * 256, 256), 256)
        hi, lo = split(gath[:, at].T)
        ph[at, :] = hi
        plo[at, :] = lo
        return carry

    lax.fori_loop(0, gath.shape[1] // 256, turn, 0)

    for d, copy in zip(range(1, CY), a_gy):
        copy.wait_recv()
        block = piv.at[rows64(lax.rem(y + CY - d, CY)), mine]
        a_gc.append(send(block, block, A_GC + d, sibling))

    for copy in s_gz:
        copy.wait_recv()
    s_gc = send(red.at[rows64(c), :], red.at[rows64(c), :], S_GC, sibling)
    for copy in a_gc:
        copy.wait_recv()
    s_gc.wait_recv()

    @pl.when(c == 1)
    def _():
        remote(head, head, H_GC, sibling).wait_recv()

    for copy in pending:
        copy.wait_send()

    @pl.when(c == 0)
    def _():
        remote(head, head, H_GC, sibling).wait_send()
        for d in range(1, CZ):
            remote(my_head, my_head, H_GZ + d - 1, to_z(d)).wait_send()
        for d in range(1, CY):
            remote(head.at[y], head.at[y], H_GY + d - 1, to_y(d)).wait_send()

    @pl.when((y == 0) & (c == 0))
    def _():
        for d in range(1, CY):
            remote(deal.at[d, rows8(z), :], head.at[d, rows8(z), :], H_Y + d - 1, to_y(d)).wait_send()

    @pl.when(root)
    def _():
        for d in range(1, CZ):
            part = deal.at[:, pl.ds(8 * d, 8), :]
            remote(part, part, H_Z + d - 1, to_z(d)).wait_send()


def update_kernel(
    info, piv_v, look, ph, plo, piv, head, red, upper, lower,
    out, lp, sk,
    vh, vl, th, tl, ut, uh, ul, fh, fl, ur,
):
    step = pl.program_id(0)
    tile = look.shape[0]
    first, x = info[0], info[1]

    @pl.when(step == 0)
    def _():
        i = lax.broadcasted_iota(jnp.int32, (NB, NB), 0)
        j = lax.broadcasted_iota(jnp.int32, (NB, NB), 1)
        low = jnp.where(i > j, lower[...], jnp.where(i == j, 1.0, 0.0))
        up = jnp.where(i <= j, upper[...], 0.0)
        u_rows = dot3(split(low), split(piv[...]))
        ur[...] = u_rows
        v = split(dot3(split(up), split(u_rows)))
        vh[...], vl[...] = v
        rows = head[...].reshape(NB, 768)
        cols = split(rows[:, 512:])
        t = rows[:, :512] - dot3(split(rows[:, 512:].T), v)
        th[...], tl[...] = split(t)
        ut[...] = up.T
        u = split(ut[pl.ds(pl.multiple_of(x * 64, 64), 64), :])
        uh[...], ul[...] = u
        fh[...], fl[...] = split(dot3(u, cols))
        sk[...] = red[0:64, :]

    at = lax.broadcasted_iota(jnp.int32, (tile, NB), 0) + (first + step * tile)
    hot32 = jnp.where(at == piv_v[...], 1.0, 0.0)
    hit = jnp.max(hot32, axis=1, keepdims=True)
    hot = hot32.astype(BF16)
    p = (ph[...], plo[...])
    plain = look[...] - dot3(p, (vh[...], vl[...]))
    moved = dot(hot, th[...]) + dot(hot, tl[...])
    out[...] = jnp.where(hit > 0.0, moved, plain)
    nt = ((1,), (1,))
    factor = dot3((uh[...], ul[...]), p, nt)
    parts = dot(jnp.concatenate([fh[...], fl[...], jnp.ones((16, NB), BF16)], 0), hot, nt)
    lp[...] = jnp.where(parts[128:129] > 0.0, parts[0:64] + parts[64:128], factor)

    @pl.when((step == 0) & (first == 0))
    def _():
        out[0:NB, :] = ur[...]
        lp[:, 0:NB] = red[64:128, :]


def on_device(panel_col, look_cols, sketch_map, upper_inv, lower_inv, pivots):
    rows, width = look_cols.shape
    panel_t = panel_col.T
    piv_row = pivots.reshape(1, NB)
    vmem = pl.BlockSpec(memory_space=pltpu.VMEM)
    smem = pl.BlockSpec(memory_space=pltpu.SMEM)
    hbm = pl.BlockSpec(memory_space=pl.ANY)
    piv, head, red, ph, plo = pl.pallas_call(
        comm_kernel,
        out_shape=(
            jax.ShapeDtypeStruct((NB, width), F32),
            jax.ShapeDtypeStruct((CY, 64, width + NB), F32),
            jax.ShapeDtypeStruct((128, NB), F32),
            jax.ShapeDtypeStruct((rows, NB), BF16),
            jax.ShapeDtypeStruct((rows, NB), BF16),
        ),
        in_specs=[smem, vmem, hbm, hbm, hbm],
        out_specs=(vmem,) * 5,
        scratch_shapes=[
            pltpu.VMEM((rows, width), F32),
            pltpu.VMEM((NB, rows), F32),
            pltpu.VMEM((NB, rows), F32),
            pltpu.VMEM((NB, width), F32),
            pltpu.VMEM((NB, 256), F32),
            pltpu.VMEM((NB, 256), F32),
            pltpu.VMEM((3, 64, 256), F32),
            pltpu.VMEM((64, 256), F32),
            pltpu.VMEM((7, 8, 256), F32),
            pltpu.VMEM((128, NB), F32),
            pltpu.VMEM((64, NB), F32),
            pltpu.VMEM((64, NB), F32),
            pltpu.VMEM((7, 8, NB), F32),
            pltpu.VMEM((4, 8, NB), F32),
            pltpu.VMEM((CY, 64, width + NB), F32),
            pltpu.SemaphoreType.DMA((8,)),
            pltpu.SemaphoreType.DMA((N_SEM,)),
            pltpu.SemaphoreType.DMA((N_SEM,)),
        ],
        compiler_params=pltpu.CompilerParams(
            collective_id=0, has_side_effects=True, vmem_limit_bytes=40 << 20
        ),
        name="exchange",
    )(pivots, piv_row, panel_t, look_cols, sketch_map)

    info = jnp.stack([lax.axis_index("row") * rows, lax.axis_index("col")]).astype(jnp.int32)
    tile = 512

    def whole(shape):
        return pl.BlockSpec(shape, lambda i: (0,) * len(shape))

    def by_row(cols):
        return pl.BlockSpec((tile, cols), lambda i: (i, 0))

    updated, lp, sk = pl.pallas_call(
        update_kernel,
        grid=(rows // tile,),
        out_shape=(
            jax.ShapeDtypeStruct((rows, width), F32),
            jax.ShapeDtypeStruct((64, rows), F32),
            jax.ShapeDtypeStruct((64, NB), F32),
        ),
        in_specs=[
            smem, whole((1, NB)), by_row(width), by_row(NB), by_row(NB),
            whole((NB, width)), whole((CY, 64, width + NB)), whole((128, NB)), whole((NB, NB)), whole((NB, NB)),
        ],
        out_specs=(by_row(width), pl.BlockSpec((64, tile), lambda i: (0, i)), whole((64, NB))),
        scratch_shapes=[
            pltpu.VMEM((NB, width), BF16),
            pltpu.VMEM((NB, width), BF16),
            pltpu.VMEM((NB, width), BF16),
            pltpu.VMEM((NB, width), BF16),
            pltpu.VMEM((NB, NB), F32),
            pltpu.VMEM((64, NB), BF16),
            pltpu.VMEM((64, NB), BF16),
            pltpu.VMEM((64, NB), BF16),
            pltpu.VMEM((64, NB), BF16),
            pltpu.VMEM((NB, width), F32),
        ],
        compiler_params=pltpu.CompilerParams(vmem_limit_bytes=32 << 20),
        name="update",
    )(info, piv_row, look_cols, ph, plo, piv, head, red, upper_inv, lower_inv)
    return lp.T, updated, sk.T


def solution(mesh):
    placed = (P("row", "col"), P("row", "col"), P(None, "row"), P(), P(), P())
    return jax.shard_map(
        on_device,
        mesh=mesh,
        in_specs=placed,
        out_specs=(P("row", "col"), P("row", "col"), P(None, "col")),
        check_vma=False,
    )
```

```python
import jax
import jax.numpy as jnp
from jax import lax
from jax.experimental import pallas as pl
from jax.experimental.pallas import tpu as pltpu
from jax.sharding import PartitionSpec as P

MESH = pl.DeviceIdType.MESH
F32, BF16 = jnp.float32, jnp.bfloat16
NB = 256
CY, CZ = 4, 8

X_RING = 0
A_CORE = 6
A_Y = 10
A_Z = 13
A_GZ = 20
A_GY = 27
A_GC = 30
S_CORE = 34
S_Z = 35
S_Y = 42
S_GZ = 45
S_GC = 52
H_X = 53
H_S = 57
H_R = 89
H_GZ = 90
H_GY = 97
H_GC = 100
N_SEM = 101
CHIPS = CY * CZ


def split(a):
    hi = a.astype(BF16)
    return hi, (a - hi.astype(F32)).astype(BF16)


def dot(a, b, dims=((1,), (0,))):
    return lax.dot_general(a, b, (dims, ((), ())), preferred_element_type=F32)


def dot3(a, b, dims=((1,), (0,))):
    (ah, al), (bh, bl) = a, b
    return dot(ah, bh, dims) + dot(al, bh, dims) + dot(ah, bl, dims)


def comm_kernel(
    pivots, piv_row, panel, look, smap,
    piv, head, phead, red, ph, plo,
    piv_s, piv_v, look_v, sm_v, gath, pick, cbuf, hsum, ybuf, zin, zbuf,
    spart, scbuf, ssum, szbuf, sybuf, deal,
    ld, ss, rs,
):
    r, x = lax.axis_index("row"), lax.axis_index("col")
    c = lax.rem(r, 2)
    y = lax.rem(lax.div(r, 2), CY)
    z = lax.div(r, 2 * CY)
    first = r * look.shape[0]

    def to_x(d):
        return (r, lax.rem(x + d + 4, 4))

    def to_y(d):
        return ((z * CY + lax.rem(y + d, CY)) * 2 + c, x)

    def to_z(d):
        return ((lax.rem(z + d, CZ) * CY + y) * 2 + c, x)

    sibling = ((z * CY + y) * 2 + 1 - c, x)

    pending = []

    def remote(src, dst, slot, device, recv_slot=None):
        return pltpu.make_async_remote_copy(
            src_ref=src, dst_ref=dst, send_sem=ss.at[slot],
            recv_sem=rs.at[slot if recv_slot is None else recv_slot],
            device_id=device, device_id_type=MESH,
        )

    def send(*args):
        copy = remote(*args)
        copy.start()
        pending.append(copy)
        return copy

    def rows8(i):
        return pl.ds(pl.multiple_of(i * 8, 8), 8)

    def rows64(i):
        return pl.ds(pl.multiple_of(i * 64, 64), 64)

    mine = pl.ds(pl.multiple_of(c * 256, 256), 256)
    other = pl.ds(pl.multiple_of((1 - c) * 256, 256), 256)
    half_cols = gath.shape[1] // 2
    halves = [pl.ds(0, half_cols), pl.ds(half_cols, half_cols)]
    own_block = rows64(x)

    load_piv = [
        pltpu.make_async_copy(pivots, piv_s, ld.at[3]),
        pltpu.make_async_copy(piv_row, piv_v, ld.at[4]),
    ]
    for copy in load_piv:
        copy.start()
    load_look = pltpu.make_async_copy(look, look_v, ld.at[0])
    load_look.start()
    load_panel = pltpu.make_async_copy(panel, gath.at[own_block, :], ld.at[1])
    load_panel.start()
    load_map = pltpu.make_async_copy(smap, sm_v, ld.at[2])
    load_map.start()

    bar = pltpu.get_barrier_semaphore()
    partners = [to_x(1), to_x(3), sibling]
    partners += [to_y(d) for d in range(1, CY)] + [to_z(d) for d in range(1, CZ)]

    def greet(device):
        pl.semaphore_signal(bar, inc=1, device_id=device, device_id_type=MESH)

    for device in partners:
        greet(device)

    @pl.when((y > 0) & (z > 0))
    def _():
        greet((c, x))

    @pl.when(r == 1)
    def _():
        for d in range(1, 4):
            greet((0, lax.rem(x + d, 4)))


    load_piv[0].wait()
    load_look.wait()

    def pick_rows(i, carry):
        for k in range(8):
            row = i * 8 + k
            local = piv_s[row] - first
            owned = (local >= 0) & (local < look_v.shape[0])
            at = jnp.where(owned, local, 0)
            pick[pl.ds(row, 1), :] = jnp.where(owned, look_v[pl.ds(at, 1), :], 0.0)
        return carry

    lax.fori_loop(0, NB // 8, pick_rows, 0)
    far = (CY - 1) * (CZ - 1)

    @pl.when(r == 0)
    def _():
        pl.semaphore_wait(bar, len(partners) + far + 3)

    @pl.when(r == 1)
    def _():
        pl.semaphore_wait(bar, len(partners) + far)

    @pl.when(r > 1)
    def _():
        pl.semaphore_wait(bar, len(partners))

    a_core = []
    for d in (1, 2, 3, 0):
        block = rows64(lax.rem(y + d, CY))
        a_core.append((d, block, send(pick.at[block, other], cbuf.at[block, :], A_CORE + d, sibling)))

    right, left = to_x(1), to_x(-1)
    ring = [
        send(panel.at[:, halves[0]], gath.at[own_block, halves[0]], X_RING, right),
        send(panel.at[:, halves[1]], gath.at[own_block, halves[1]], X_RING + 2, left),
        send(panel.at[:, halves[1]], gath.at[own_block, halves[1]], X_RING + 1, right),
        send(panel.at[:, halves[0]], gath.at[own_block, halves[0]], X_RING + 3, left),
    ]

    def share(ref, q):
        return ref.at[rows8(lax.rem(q, CY) * CZ + lax.div(q, CY)), :]

    def deal_out(src, dst):
        def one(q, carry):
            remote(share(src, q), share(dst, q), H_S + q, (2 * q + c, x), H_R).start()
            return carry

        lax.fori_loop(1, CHIPS, one, 0)

    def dealt(src, dst):
        def one(q, carry):
            remote(share(src, q), share(dst, q), H_S + q, (2 * q + c, x), H_R).wait_send()
            return carry

        lax.fori_loop(1, CHIPS, one, 0)

    own_head = pltpu.make_async_copy(look.at[pl.ds(0, 8), :], head.at[pl.ds(0, 8), :], ld.at[5])

    @pl.when(r == 0)
    def _():
        for to in range(4):
            remote(panel.at[:, pl.ds(0, NB)], deal.at[rows64(x), :], H_X + to, (1, to), H_X + x).start()
        own_head.start()
        deal_out(look, head)

    a_y = []
    for d, block, copy in a_core:
        copy.wait_recv()
        hsum[block, :] = pick[block, mine] + cbuf[block, :]
        if d:
            a_y.append(send(hsum.at[block, :], ybuf.at[d - 1], A_Y + d - 1, to_y(d)))

    @pl.when(r == 1)
    def _():
        for q in range(4):
            block = deal.at[pl.ds(64 * q, 64), :]
            remote(block, block, H_X + q, sibling).wait_recv()
        phead[pl.ds(0, 8), :] = deal[pl.ds(0, 8), :]
        deal_out(deal, phead)

    load_panel.wait()
    load_piv[1].wait()
    load_map.wait()
    spart[...] = jnp.zeros_like(spart)
    tile = 512

    def small(i, carry):
        cols = pl.ds(pl.multiple_of(i * tile, tile), tile)
        p = gath[own_block, cols]
        p1, p2 = split(p)
        p3 = (p - p1.astype(F32) - p2.astype(F32)).astype(BF16)
        mh, ml = split(sm_v[:, cols])
        nt = ((1,), (1,))
        both = dot(jnp.concatenate([p1, p2], 0), mh, nt)
        spart[0:64, :] += both[0:64] + both[64:128] + dot(p1, ml, nt)
        at = lax.broadcasted_iota(jnp.int32, (tile, NB), 0) + (first + i * tile)
        hot = jnp.where(at == piv_v[...], 1.0, 0.0).astype(BF16)
        three = dot(jnp.concatenate([p1, p2, p3], 0), hot)
        spart[64:128, :] += three[0:64] + three[64:128] + three[128:192]
        return carry

    lax.fori_loop(0, gath.shape[1] // tile, small, 0)
    s_core = send(spart.at[rows64(1 - c), :], scbuf, S_CORE, sibling)

    for copy in a_y:
        copy.wait_recv()
    zin[...] = hsum[rows64(y), :] + ybuf[0] + ybuf[1] + ybuf[2]
    a_z = [send(zin.at[rows8(lax.rem(z + d, CZ)), :], zbuf.at[d - 1], A_Z + d - 1, to_z(d)) for d in range(1, CZ)]

    s_core.wait_recv()
    ssum[...] = spart[rows64(c), :] + scbuf[...]
    s_z = [send(ssum.at[rows8(lax.rem(z + d, CZ)), :], szbuf.at[d - 1], S_Z + d - 1, to_z(d)) for d in range(1, CZ)]

    at_mine = rows8(y * CZ + z)
    own_rows = rows64(y)

    def by_core(stage):
        pl.when(c == 0)(lambda: stage(head))
        pl.when(c == 1)(lambda: stage(phead))

    def head_over_z(buf):
        own = buf.at[at_mine, :]

        @pl.when(r > 1)
        def _():
            remote(own, own, H_R, sibling).wait_recv()

        for d in range(1, CZ):
            remote(own, own, H_GZ + d - 1, to_z(d)).start()

    def head_over_y(buf):
        own = buf.at[at_mine, :]
        for d in range(1, CZ):
            remote(own, own, H_GZ + d - 1, to_z(d)).wait_recv()
        for d in range(1, CY):
            remote(buf.at[own_rows, :], buf.at[own_rows, :], H_GY + d - 1, to_y(d)).start()

    def head_over_core(buf):
        own = buf.at[own_rows, :]
        for d in range(1, CY):
            remote(own, own, H_GY + d - 1, to_y(d)).wait_recv()
        remote(buf, buf, H_GC, sibling).start()

    def head_left(buf):
        own = buf.at[at_mine, :]
        for d in range(1, CZ):
            remote(own, own, H_GZ + d - 1, to_z(d)).wait_send()
        own = buf.at[own_rows, :]
        for d in range(1, CY):
            remote(own, own, H_GY + d - 1, to_y(d)).wait_send()
        remote(buf, buf, H_GC, sibling).wait_send()

    pl.when(r == 0)(own_head.wait)
    by_core(head_over_z)

    ring[0].wait_recv()
    block = gath.at[rows64(lax.rem(x + 3, 4)), halves[0]]
    ring.append(send(block, block, X_RING + 4, right))
    ring[1].wait_recv()
    block = gath.at[rows64(lax.rem(x + 1, 4)), halves[1]]
    ring.append(send(block, block, X_RING + 5, left))

    for copy in a_z:
        copy.wait_recv()
    total = zin[rows8(z), :]
    for d in range(1, CZ):
        total = total + zbuf[d - 1]
    piv[at_mine, mine] = total
    chunk = piv.at[at_mine, mine]
    a_gz = [send(chunk, chunk, A_GZ + d - 1, to_z(d)) for d in range(1, CZ)]

    by_core(head_over_y)

    for copy in s_z:
        copy.wait_recv()
    total = ssum[rows8(z), :]
    for d in range(1, CZ):
        total = total + szbuf[d - 1]
    sybuf[y] = total
    s_y = [send(sybuf.at[y], sybuf.at[y], S_Y + d - 1, to_y(d)) for d in range(1, CY)]

    for copy in a_gz:
        copy.wait_recv()
    quarter = piv.at[rows64(y), mine]
    a_gy = [send(quarter, quarter, A_GY + d - 1, to_y(d)) for d in range(1, CY)]
    a_gc = [send(quarter, quarter, A_GC, sibling)]

    for copy in s_y:
        copy.wait_recv()
    at_small = pl.ds(pl.multiple_of(c * 64 + z * 8, 8), 8)
    red[at_small, :] = sybuf[0] + sybuf[1] + sybuf[2] + sybuf[3]
    s_gz = [send(red.at[at_small, :], red.at[at_small, :], S_GZ + d - 1, to_z(d)) for d in range(1, CZ)]

    by_core(head_over_core)

    for copy in ring[2:]:
        copy.wait_recv()

    def turn(i, carry):
        at = pl.ds(pl.multiple_of(i * 256, 256), 256)
        hi, lo = split(gath[:, at].T)
        ph[at, :] = hi
        plo[at, :] = lo
        return carry

    lax.fori_loop(0, gath.shape[1] // 256, turn, 0)

    for d, copy in zip(range(1, CY), a_gy):
        copy.wait_recv()
        block = piv.at[rows64(lax.rem(y + CY - d, CY)), mine]
        a_gc.append(send(block, block, A_GC + d, sibling))

    for copy in s_gz:
        copy.wait_recv()
    s_gc = send(red.at[rows64(c), :], red.at[rows64(c), :], S_GC, sibling)
    for copy in a_gc:
        copy.wait_recv()
    s_gc.wait_recv()

    @pl.when(c == 0)
    def _():
        remote(phead, phead, H_GC, sibling).wait_recv()

    @pl.when(c == 1)
    def _():
        remote(head, head, H_GC, sibling).wait_recv()

    for copy in pending:
        copy.wait_send()
    by_core(head_left)

    @pl.when(r == 0)
    def _():
        for to in range(4):
            remote(panel.at[:, pl.ds(0, NB)], deal.at[rows64(x), :], H_X + to, (1, to), H_X + x).wait_send()
        dealt(look, head)

    @pl.when(r == 1)
    def _():
        dealt(deal, phead)


def update_kernel(
    info, piv_v, look, ph, plo, piv, head, phead, red, upper, lower,
    out, lp, sk,
    vh, vl, th, tl, ut, uh, ul, fh, fl, ur,
):
    step = pl.program_id(0)
    tile = look.shape[0]
    first, x = info[0], info[1]

    @pl.when(step == 0)
    def _():
        i = lax.broadcasted_iota(jnp.int32, (NB, NB), 0)
        j = lax.broadcasted_iota(jnp.int32, (NB, NB), 1)
        low = jnp.where(i > j, lower[...], jnp.where(i == j, 1.0, 0.0))
        up = jnp.where(i <= j, upper[...], 0.0)
        u_rows = dot3(split(low), split(piv[...]))
        ur[...] = u_rows
        v = split(dot3(split(up), split(u_rows)))
        vh[...], vl[...] = v
        cols = split(phead[...])
        t = head[...] - dot3(split(phead[...].T), v)
        th[...], tl[...] = split(t)
        ut[...] = up.T
        u = split(ut[pl.ds(pl.multiple_of(x * 64, 64), 64), :])
        uh[...], ul[...] = u
        fh[...], fl[...] = split(dot3(u, cols))
        sk[...] = red[0:64, :]

    at = lax.broadcasted_iota(jnp.int32, (tile, NB), 0) + (first + step * tile)
    hot32 = jnp.where(at == piv_v[...], 1.0, 0.0)
    hit = jnp.max(hot32, axis=1, keepdims=True)
    hot = hot32.astype(BF16)
    p = (ph[...], plo[...])
    plain = look[...] - dot3(p, (vh[...], vl[...]))
    moved = dot(hot, th[...]) + dot(hot, tl[...])
    out[...] = jnp.where(hit > 0.0, moved, plain)
    nt = ((1,), (1,))
    factor = dot3((uh[...], ul[...]), p, nt)
    parts = dot(jnp.concatenate([fh[...], fl[...], jnp.ones((16, NB), BF16)], 0), hot, nt)
    lp[...] = jnp.where(parts[128:129] > 0.0, parts[0:64] + parts[64:128], factor)

    @pl.when((step == 0) & (first == 0))
    def _():
        out[0:NB, :] = ur[...]
        lp[:, 0:NB] = red[64:128, :]


def on_device(panel_col, look_cols, sketch_map, upper_inv, lower_inv, pivots):
    rows, width = look_cols.shape
    panel_t = panel_col.T
    piv_row = pivots.reshape(1, NB)
    vmem = pl.BlockSpec(memory_space=pltpu.VMEM)
    smem = pl.BlockSpec(memory_space=pltpu.SMEM)
    hbm = pl.BlockSpec(memory_space=pltpu.HBM)
    piv, head, phead, red, ph, plo = pl.pallas_call(
        comm_kernel,
        out_shape=(
            jax.ShapeDtypeStruct((NB, width), F32),
            jax.ShapeDtypeStruct((NB, width), F32),
            jax.ShapeDtypeStruct((NB, NB), F32),
            jax.ShapeDtypeStruct((128, NB), F32),
            jax.ShapeDtypeStruct((rows, NB), BF16),
            jax.ShapeDtypeStruct((rows, NB), BF16),
        ),
        in_specs=[hbm] * 5,
        out_specs=(vmem,) * 6,
        scratch_shapes=[
            pltpu.SMEM((NB,), jnp.int32),
            pltpu.VMEM((1, NB), jnp.int32),
            pltpu.VMEM((rows, width), F32),
            pltpu.VMEM((NB, rows), F32),
            pltpu.VMEM((NB, rows), F32),
            pltpu.VMEM((NB, width), F32),
            pltpu.VMEM((NB, 256), F32),
            pltpu.VMEM((NB, 256), F32),
            pltpu.VMEM((3, 64, 256), F32),
            pltpu.VMEM((64, 256), F32),
            pltpu.VMEM((7, 8, 256), F32),
            pltpu.VMEM((128, NB), F32),
            pltpu.VMEM((64, NB), F32),
            pltpu.VMEM((64, NB), F32),
            pltpu.VMEM((7, 8, NB), F32),
            pltpu.VMEM((4, 8, NB), F32),
            pltpu.VMEM((NB, NB), F32),
            pltpu.SemaphoreType.DMA((8,)),
            pltpu.SemaphoreType.DMA((N_SEM,)),
            pltpu.SemaphoreType.DMA((N_SEM,)),
        ],
        compiler_params=pltpu.CompilerParams(
            collective_id=0, has_side_effects=True, vmem_limit_bytes=40 << 20
        ),
        name="exchange",
    )(*[pltpu.with_memory_space_constraint(a, pltpu.HBM) for a in (pivots, piv_row, panel_t, look_cols, sketch_map)])

    info = jnp.stack([lax.axis_index("row") * rows, lax.axis_index("col")]).astype(jnp.int32)
    tile = 512

    def whole(shape):
        return pl.BlockSpec(shape, lambda i: (0,) * len(shape))

    def by_row(cols):
        return pl.BlockSpec((tile, cols), lambda i: (i, 0))

    updated, lp, sk = pl.pallas_call(
        update_kernel,
        grid=(rows // tile,),
        out_shape=(
            jax.ShapeDtypeStruct((rows, width), F32),
            jax.ShapeDtypeStruct((64, rows), F32),
            jax.ShapeDtypeStruct((64, NB), F32),
        ),
        in_specs=[
            smem, whole((1, NB)), by_row(width), by_row(NB), by_row(NB),
            whole((NB, width)), whole((NB, width)), whole((NB, NB)), whole((128, NB)), whole((NB, NB)), whole((NB, NB)),
        ],
        out_specs=(by_row(width), pl.BlockSpec((64, tile), lambda i: (0, i)), whole((64, NB))),
        scratch_shapes=[
            pltpu.VMEM((NB, width), BF16),
            pltpu.VMEM((NB, width), BF16),
            pltpu.VMEM((NB, width), BF16),
            pltpu.VMEM((NB, width), BF16),
            pltpu.VMEM((NB, NB), F32),
            pltpu.VMEM((64, NB), BF16),
            pltpu.VMEM((64, NB), BF16),
            pltpu.VMEM((64, NB), BF16),
            pltpu.VMEM((64, NB), BF16),
            pltpu.VMEM((NB, width), F32),
        ],
        compiler_params=pltpu.CompilerParams(vmem_limit_bytes=32 << 20),
        name="update",
    )(info, piv_row, look_cols, ph, plo, piv, head, phead, red, upper_inv, lower_inv)
    return lp.T, updated, sk.T


def solution(mesh):
    placed = (P("row", "col"), P("row", "col"), P(None, "row"), P(), P(), P())
    return jax.shard_map(
        on_device,
        mesh=mesh,
        in_specs=placed,
        out_specs=(P("row", "col"), P("row", "col"), P(None, "col")),
        check_vma=False,
    )
```

```python
import jax
import jax.numpy as jnp
from jax import lax
from jax.experimental import pallas as pl
from jax.experimental.pallas import tpu as pltpu
from jax.sharding import PartitionSpec as P

MESH = pl.DeviceIdType.MESH
F32, BF16 = jnp.float32, jnp.bfloat16
NB = 256
CY, CZ = 4, 8
CHIPS = CY * CZ

X_RING = 0
A_CORE = 6
A_Y = 10
A_Z = 14
A_GZ = 22
A_GY = 42
A_GC = 74
S_CORE = 78
S_Y = 79
S_Z = 83
S_GY = 91
S_GC = 95
H_X = 96
H_S = 100
H_R = 132
H_GZ = 133
H_GY = 141
H_GC = 173
N_SEM = 177

FAR_Z = (4, 3, 5, 2, 6, 1, 7)
NEAR_Z = (1, 7, 2, 6, 3, 5, 4)


def split(a):
    hi = a.astype(BF16)
    return hi, (a - hi.astype(F32)).astype(BF16)


def dot(a, b, dims=((1,), (0,))):
    return lax.dot_general(a, b, (dims, ((), ())), preferred_element_type=F32)


def dot3(a, b):
    (ah, al), (bh, bl) = a, b
    return dot(ah, bh) + dot(al, bh) + dot(ah, bl)


def exchange_kernel(
    pivots, piv_row, panel, look, smap, upper, lower,
    left_ref, va, vb, ur, lp, sk,
    piv_s, piv_v, look_v, sm_v, up_v, low_v, gath, hot_t, hit,
    pick, cbuf, hsum, ybuf, zin, zbuf, piv, head, phead, deal,
    spart, scbuf, ssum, sybuf, szbuf, red,
    ld, ss, rs,
):
    r, x = lax.axis_index("row"), lax.axis_index("col")
    c = lax.rem(r, 2)
    y = lax.rem(lax.div(r, 2), CY)
    z = lax.div(r, 2 * CY)
    rows = look.shape[0]
    first = r * rows

    def chip(dy, dz):
        return ((lax.rem(z + dz, CZ) * CY + lax.rem(y + dy, CY)) * 2 + c, x)

    def to_x(d):
        return (r, lax.rem(x + d + 4, 4))

    sibling = ((z * CY + y) * 2 + 1 - c, x)
    pending = []

    def remote(src, dst, slot, device, recv_slot=None):
        return pltpu.make_async_remote_copy(
            src_ref=src, dst_ref=dst, send_sem=ss.at[slot],
            recv_sem=rs.at[slot if recv_slot is None else recv_slot],
            device_id=device, device_id_type=MESH,
        )

    def send(*args):
        copy = remote(*args)
        copy.start()
        pending.append(copy)
        return copy

    def block_of(i, n):
        return pl.ds(pl.multiple_of(i * n, n), n)

    def rows_of(dy, dz):
        return block_of(lax.rem(y + dy, CY) * CZ + lax.rem(z + dz, CZ), 8)

    mine, other = block_of(c, 256), block_of(1 - c, 256)
    half_cols = rows // 2
    halves = [pl.ds(0, half_cols), pl.ds(half_cols, half_cols)]
    own_block = block_of(x, 64)

    loads = {}
    for i, (name, src, dst) in enumerate(
        (
            ("piv_s", pivots, piv_s),
            ("look", look, look_v),
            ("piv_v", piv_row, piv_v),
            ("panel", panel, gath.at[own_block, :]),
            ("map", smap, sm_v),
            ("upper", upper, up_v),
            ("lower", lower, low_v),
        )
    ):
        loads[name] = pltpu.make_async_copy(src, dst, ld.at[i])
        loads[name].start()

    bar = pltpu.get_barrier_semaphore()

    def greet(device):
        pl.semaphore_signal(bar, inc=1, device_id=device, device_id_type=MESH)

    partners = [chip(d, 0) for d in range(1, CY)] + [chip(0, d) for d in range(1, CZ)]
    partners += [to_x(1), to_x(3), sibling]
    for device in partners:
        greet(device)

    @pl.when((y > 0) & (z > 0))
    def _():
        greet((c, x))

    @pl.when(r == 1)
    def _():
        for d in range(1, 4):
            greet((0, lax.rem(x + d, 4)))

    loads["piv_s"].wait()
    loads["look"].wait()

    def pick_rows(i, carry):
        for k in range(8):
            row = i * 8 + k
            local = piv_s[row] - first
            owned = (local >= 0) & (local < rows)
            at = jnp.where(owned, local, 0)
            pick[pl.ds(row, 1), :] = jnp.where(owned, look_v[pl.ds(at, 1), :], 0.0)
        return carry

    lax.fori_loop(0, NB // 8, pick_rows, 0)

    far = (CY - 1) * (CZ - 1)

    @pl.when(r == 0)
    def _():
        pl.semaphore_wait(bar, len(partners) + far + 3)

    @pl.when(r == 1)
    def _():
        pl.semaphore_wait(bar, len(partners) + far)

    @pl.when(r > 1)
    def _():
        pl.semaphore_wait(bar, len(partners))

    a_core = []
    for d in (2, 1, 3, 0):
        block = block_of(lax.rem(y + d, CY), 64)
        a_core.append((d, block, send(pick.at[block, other], cbuf.at[block, :], A_CORE + d, sibling)))

    def share(ref, q):
        return ref.at[block_of(lax.rem(q, CY) * CZ + lax.div(q, CY), 8), :]

    def shares(src, dst, act):
        def one(q, carry):
            act(remote(share(src, q), share(dst, q), H_S + q, (2 * q + c, x), H_R))
            return carry

        lax.fori_loop(1, CHIPS, one, 0)

    def columns(to):
        return remote(panel.at[:, pl.ds(0, NB)], deal.at[own_block, :], H_X + to, (1, to), H_X + x)

    own_head = pltpu.make_async_copy(look.at[pl.ds(0, 8), :], head.at[pl.ds(0, 8), :], ld.at[7])

    @pl.when(r == 0)
    def _():
        for to in range(4):
            columns(to).start()
        own_head.start()
        shares(look, head, lambda copy: copy.start())

    right, left = to_x(1), to_x(3)
    ring = [
        send(panel.at[:, halves[0]], gath.at[own_block, halves[0]], X_RING, right),
        send(panel.at[:, halves[1]], gath.at[own_block, halves[1]], X_RING + 2, left),
        send(panel.at[:, halves[1]], gath.at[own_block, halves[1]], X_RING + 1, right),
        send(panel.at[:, halves[0]], gath.at[own_block, halves[0]], X_RING + 3, left),
    ]

    a_y = []
    for d, block, copy in a_core:
        copy.wait_recv()
        hsum[block, :] = pick[block, mine] + cbuf[block, :]
        if d:
            a_y.append(send(hsum.at[block, :], ybuf.at[d - 1], A_Y + d, chip(d, 0)))

    @pl.when(r == 1)
    def _():
        for q in range(4):
            block = deal.at[pl.ds(64 * q, 64), :]
            remote(block, block, H_X + q, sibling).wait_recv()
        phead[pl.ds(0, 8), :] = deal[pl.ds(0, 8), :]
        shares(deal, phead, lambda copy: copy.start())

    loads["panel"].wait()
    loads["piv_v"].wait()
    loads["map"].wait()
    spart[...] = jnp.zeros_like(spart)
    tile = 256
    wide = jnp.broadcast_to(piv_v[...], (NB, NB))
    tall = wide.T

    def small(i, carry):
        cols = block_of(i, tile)
        p = gath[own_block, cols]
        p1, p2 = split(p)
        p3 = (p - p1.astype(F32) - p2.astype(F32)).astype(BF16)
        mh, ml = split(sm_v[:, cols])
        nt = ((1,), (1,))
        both = dot(jnp.concatenate([p1, p2], 0), mh, nt)
        spart[0:64, :] += both[0:64] + both[64:128] + dot(p1, ml, nt)
        start = first + i * tile
        at = lax.broadcasted_iota(jnp.int32, (tile, NB), 0) + start
        hot = jnp.where(at == wide, 1.0, 0.0).astype(BF16)
        left_ref[cols, 512:768] = hot
        at = lax.broadcasted_iota(jnp.int32, (NB, tile), 1) + start
        turned = jnp.where(at == tall, 1.0, 0.0)
        hot_t[:, cols] = turned.astype(BF16)
        hit[:, cols] = jnp.broadcast_to(jnp.max(turned, axis=0, keepdims=True), (8, tile))
        three = dot(jnp.concatenate([p1, p2, p3], 0), hot)
        spart[64:128, :] += three[0:64] + three[64:128] + three[128:192]
        return carry

    lax.fori_loop(0, rows // tile, small, 0)
    s_core = send(spart.at[block_of(1 - c, 64), :], scbuf, S_CORE, sibling)
    s_core.wait_recv()
    ssum[...] = spart[block_of(c, 64), :] + scbuf[...]
    s_y = [send(ssum.at[block_of(lax.rem(y + d, CY), 16), :], sybuf.at[d - 1], S_Y + d, chip(d, 0)) for d in range(1, CY)]

    for copy in a_y:
        copy.wait_recv()
    zin[...] = hsum[block_of(y, 64), :] + ybuf[0] + ybuf[1] + ybuf[2]
    a_z = [send(zin.at[block_of(lax.rem(z + d, CZ), 8), :], zbuf.at[d - 1], A_Z + d, chip(0, d)) for d in FAR_Z]

    own = rows_of(0, 0)

    def by_core(stage):
        pl.when(c == 0)(lambda: stage(head))
        pl.when(c == 1)(lambda: stage(phead))

    def over_z(buf, d):
        return remote(buf.at[own, :], buf.at[own, :], H_GZ + d, chip(0, d))

    def over_y(buf, d, e):
        part = buf.at[rows_of(0, CZ - e), :]
        return remote(part, part, H_GY + d * CZ + e, chip(d, 0))

    def over_core(buf, d):
        part = buf.at[block_of(lax.rem(y + d, CY), 64), :]
        return remote(part, part, H_GC + d, sibling)

    def head_over_z(buf):
        @pl.when(r > 1)
        def _():
            remote(buf.at[own, :], buf.at[own, :], H_R, sibling).wait_recv()

        for d in FAR_Z:
            over_z(buf, d).start()
        for d in range(1, CY):
            over_y(buf, d, 0).start()

    def head_over_y(buf):
        for e in NEAR_Z:
            over_z(buf, e).wait_recv()
            for d in (2, 1, 3):
                over_y(buf, d, e).start()
        over_core(buf, 0).start()

    def head_over_core(buf):
        for d in (1, 3, 2):
            for e in range(CZ):
                over_y(buf, CY - d, e).wait_recv()
            over_core(buf, d).start()

    def head_arrived(buf):
        for d in range(CY):
            over_core(buf, d).wait_recv()

    def head_left(buf):
        for d in range(1, CZ):
            over_z(buf, d).wait_send()
        for d in range(1, CY):
            for e in range(CZ):
                over_y(buf, d, e).wait_send()
        for d in range(CY):
            over_core(buf, d).wait_send()

    pl.when(r == 0)(own_head.wait)
    by_core(head_over_z)

    for copy in s_y:
        copy.wait_recv()
    szbuf[z] = ssum[block_of(y, 16), :] + sybuf[0] + sybuf[1] + sybuf[2]
    s_z = [send(szbuf.at[z], szbuf.at[z], S_Z + d, chip(0, d)) for d in FAR_Z]

    ring[0].wait_recv()
    block = gath.at[block_of(lax.rem(x + 3, 4), 64), halves[0]]
    ring.append(send(block, block, X_RING + 4, right))
    ring[1].wait_recv()
    block = gath.at[block_of(lax.rem(x + 1, 4), 64), halves[1]]
    ring.append(send(block, block, X_RING + 5, left))

    for copy in a_z:
        copy.wait_recv()
    total = zin[block_of(z, 8), :]
    for d in range(1, CZ):
        total = total + zbuf[d - 1]
    piv[own, mine] = total
    a_gz = {d: send(piv.at[own, mine], piv.at[own, mine], A_GZ + d, chip(0, d)) for d in FAR_Z}
    a_gy = {}

    def a_over_y(e):
        part = piv.at[rows_of(0, CZ - e), mine]
        for d in (2, 1, 3):
            a_gy[d, e] = send(part, part, A_GY + d * CZ + e, chip(d, 0))

    a_over_y(0)
    by_core(head_over_y)
    for e in NEAR_Z:
        a_gz[e].wait_recv()
        a_over_y(e)
    a_gc = []
    for d in (0, 1, 3, 2):
        for e in range(CZ):
            if d:
                a_gy[CY - d, e].wait_recv()
        part = piv.at[block_of(lax.rem(y + d, CY), 64), mine]
        a_gc.append(send(part, part, A_GC + d, sibling))

    for copy in s_z:
        copy.wait_recv()
    total = szbuf[0]
    for q in range(1, CZ):
        total = total + szbuf[q]
    at_small = block_of(c * CY + y, 16)
    red[at_small, :] = total
    s_gy = [send(red.at[at_small, :], red.at[at_small, :], S_GY + d, chip(d, 0)) for d in range(1, CY)]

    loads["upper"].wait()
    loads["lower"].wait()
    i = lax.broadcasted_iota(jnp.int32, (NB, NB), 0)
    j = lax.broadcasted_iota(jnp.int32, (NB, NB), 1)
    low = split(jnp.where(i > j, low_v[...], jnp.where(i == j, 1.0, 0.0)))
    up = jnp.where(i <= j, up_v[...], 0.0)
    low_v[...] = up.T
    u = split(low_v[own_block, :])
    both_u = jnp.concatenate(u, 0)
    for copy in a_gc:
        copy.wait_recv()
    u_rows = dot3(low, split(piv[...]))
    ur[...] = u_rows
    vh, vl = split(dot3(split(up), split(u_rows)))
    va[0:256, :] = -vh
    va[256:512, :] = -vh
    vb[0:256, :] = -vl

    by_core(head_over_core)

    for copy in ring[2:]:
        copy.wait_recv()

    def turn(i, carry):
        at = block_of(i, 256)
        kept = jnp.where(hit[0:1, at] > 0.0, 0.0, gath[:, at])
        hi, lo = split(kept)
        pre = dot(both_u, hi)
        lp[:, at] = pre[0:64] + pre[64:128] + dot(u[0], lo)
        hi, lo = split(kept.T)
        left_ref[at, 0:256] = lo
        left_ref[at, 256:512] = hi
        return carry

    lax.fori_loop(0, rows // 256, turn, 0)

    for copy in s_gy:
        copy.wait_recv()
    part = red.at[block_of(c, 64), :]
    s_gc = send(part, part, S_GC, sibling)

    pl.when(c == 0)(lambda: head_arrived(phead))
    pl.when(c == 1)(lambda: head_arrived(head))
    moved = (head[...] - piv[...]) - dot3(split(phead[...].T), (vh, vl))
    dh, dl = split(moved)
    va[512:768, :] = dh
    vb[256:512, :] = dl
    both_f = jnp.concatenate(split(dot3(u, split(phead[...]))), 0)

    def moved_factor(i, carry):
        at = block_of(i, 256)
        add = dot(both_f, hot_t[:, at])
        lp[:, at] += add[0:64] + add[64:128]
        return carry

    lax.fori_loop(0, rows // 256, moved_factor, 0)
    s_gc.wait_recv()
    sk[...] = red[0:64, :]

    @pl.when(r == 0)
    def _():
        lp[:, 0:NB] = red[64:128, :]

    for copy in pending:
        copy.wait_send()
    by_core(head_left)

    @pl.when(r == 0)
    def _():
        for to in range(4):
            columns(to).wait_send()
        shares(look, head, lambda copy: copy.wait_send())

    @pl.when(r == 1)
    def _():
        shares(deal, phead, lambda copy: copy.wait_send())


def update_kernel(first, look, left_ref, va, vb, ur, lp, sk, out, lp_out, sk_out, buf, sem, small_sem):
    tile = buf.shape[1]
    steps = buf.shape[0]
    small = [
        pltpu.make_async_copy(lp, lp_out, small_sem.at[0]),
        pltpu.make_async_copy(sk, sk_out, small_sem.at[1]),
    ]
    for copy in small:
        copy.start()

    def block(i):
        return pl.ds(pl.multiple_of(i * tile, tile), tile)

    def write(i):
        return pltpu.make_async_copy(buf.at[i], out.at[block(i), :], sem.at[i])

    def step(i, carry):
        at = block(i)
        buf[i] = look[at, :] + dot(left_ref[at, :], va[...]) + dot(left_ref[at, 256:768], vb[...])

        @pl.when((i == 0) & (first[0] == 0))
        def _():
            buf[0, 0:NB, :] = ur[...]

        write(i).start()
        return carry

    lax.fori_loop(0, steps, step, 0)
    for copy in small:
        copy.wait()
    for i in range(steps):
        write(i).wait()


def on_device(panel_col, look_cols, sketch_map, upper_inv, lower_inv, pivots):
    rows, width = look_cols.shape
    panel_t = panel_col.T
    piv_row = pivots.reshape(1, NB)
    vmem = pl.BlockSpec(memory_space=pltpu.VMEM)
    hbm = pl.BlockSpec(memory_space=pltpu.HBM)
    inputs = [
        pltpu.with_memory_space_constraint(a, pltpu.HBM)
        for a in (pivots, piv_row, panel_t, look_cols, sketch_map, upper_inv, lower_inv)
    ]
    results = pl.pallas_call(
        exchange_kernel,
        out_shape=(
            jax.ShapeDtypeStruct((rows, 3 * NB), BF16),
            jax.ShapeDtypeStruct((3 * NB, width), BF16),
            jax.ShapeDtypeStruct((2 * NB, width), BF16),
            jax.ShapeDtypeStruct((NB, width), F32),
            jax.ShapeDtypeStruct((64, rows), F32),
            jax.ShapeDtypeStruct((64, NB), F32),
        ),
        in_specs=[hbm] * len(inputs),
        out_specs=(vmem,) * 6,
        scratch_shapes=[
            pltpu.SMEM((NB,), jnp.int32),
            pltpu.VMEM((1, NB), jnp.int32),
            pltpu.VMEM((rows, width), F32),
            pltpu.VMEM((NB, rows), F32),
            pltpu.VMEM((NB, NB), F32),
            pltpu.VMEM((NB, NB), F32),
            pltpu.VMEM((NB, rows), F32),
            pltpu.VMEM((NB, rows), BF16),
            pltpu.VMEM((8, rows), F32),
            pltpu.VMEM((NB, width), F32),
            pltpu.VMEM((NB, 256), F32),
            pltpu.VMEM((NB, 256), F32),
            pltpu.VMEM((3, 64, 256), F32),
            pltpu.VMEM((64, 256), F32),
            pltpu.VMEM((7, 8, 256), F32),
            pltpu.VMEM((NB, width), F32),
            pltpu.VMEM((NB, width), F32),
            pltpu.VMEM((NB, NB), F32),
            pltpu.VMEM((NB, NB), F32),
            pltpu.VMEM((128, NB), F32),
            pltpu.VMEM((64, NB), F32),
            pltpu.VMEM((64, NB), F32),
            pltpu.VMEM((3, 16, NB), F32),
            pltpu.VMEM((CZ, 16, NB), F32),
            pltpu.VMEM((128, NB), F32),
            pltpu.SemaphoreType.DMA((8,)),
            pltpu.SemaphoreType.DMA((N_SEM,)),
            pltpu.SemaphoreType.DMA((N_SEM,)),
        ],
        compiler_params=pltpu.CompilerParams(
            collective_id=0, has_side_effects=True, vmem_limit_bytes=36 << 20
        ),
        name="exchange",
    )(*inputs)

    first = (lax.axis_index("row") * rows).astype(jnp.int32).reshape(1)
    tile = 256
    updated, lp, sk = pl.pallas_call(
        update_kernel,
        out_shape=(
            jax.ShapeDtypeStruct((rows, width), F32),
            jax.ShapeDtypeStruct((64, rows), F32),
            jax.ShapeDtypeStruct((64, NB), F32),
        ),
        in_specs=[pl.BlockSpec(memory_space=pltpu.SMEM)] + [vmem] * 7,
        out_specs=(hbm,) * 3,
        scratch_shapes=[
            pltpu.VMEM((rows // tile, tile, width), F32),
            pltpu.SemaphoreType.DMA((rows // tile,)),
            pltpu.SemaphoreType.DMA((2,)),
        ],
        compiler_params=pltpu.CompilerParams(vmem_limit_bytes=32 << 20),
        name="update",
    )(first, look_cols, *results)
    return lp.T, updated, sk.T


def solution(mesh):
    placed = (P("row", "col"), P("row", "col"), P(None, "row"), P(), P(), P())
    return jax.shard_map(
        on_device,
        mesh=mesh,
        in_specs=placed,
        out_specs=(P("row", "col"), P("row", "col"), P(None, "col")),
        check_vma=False,
    )
```

```python
import jax
import jax.numpy as jnp
from jax import lax
from jax.experimental import pallas as pl
from jax.experimental.pallas import tpu as pltpu
from jax.sharding import PartitionSpec as P

MESH = pl.DeviceIdType.MESH
F32, BF16 = jnp.float32, jnp.bfloat16
NB = 256
CY, CZ = 4, 8
CHIPS = CY * CZ

X_RING = 0
A_CORE = 6
A_Y = 10
A_Z = 18
A_GZ = 26
A_GY = 42
A_GC = 74
S_CORE = 78
S_Y = 79
S_Z = 83
S_GY = 91
S_GC = 95
H_X = 96
H_S = 100
H_R = 132
H_GZ = 133
H_GY = 141
H_GC = 173
N_SEM = 177

FAR_Z = (4, 3, 5, 2, 6, 1, 7)
NEAR_Z = (1, 7, 2, 6, 3, 5, 4)


def split(a):
    hi = a.astype(BF16)
    return hi, (a - hi.astype(F32)).astype(BF16)


def dot(a, b, dims=((1,), (0,))):
    return lax.dot_general(a, b, (dims, ((), ())), preferred_element_type=F32)


def dot3(a, b):
    (ah, al), (bh, bl) = a, b
    return dot(ah, bh) + dot(al, bh) + dot(ah, bl)


def exchange_kernel(
    pivots, piv_row, panel, look, smap, upper, lower,
    left_ref, va, vb, ur, lp, sk,
    piv_s, piv_v, look_v, sm_v, up_v, low_v, gath, hot_t, hit,
    pick, cbuf, hsum, ybuf, zin, zbuf, piv, head, phead, deal,
    spart, scbuf, ssum, sybuf, szbuf, red, lowh, lowl, mulh, mull, both_u,
    ld, ss, rs,
):
    r, x = lax.axis_index("row"), lax.axis_index("col")
    c = lax.rem(r, 2)
    y = lax.rem(lax.div(r, 2), CY)
    z = lax.div(r, 2 * CY)
    rows = look.shape[0]
    first = r * rows

    def chip(dy, dz):
        return ((lax.rem(z + dz, CZ) * CY + lax.rem(y + dy, CY)) * 2 + c, x)

    def to_x(d):
        return (r, lax.rem(x + d + 4, 4))

    sibling = ((z * CY + y) * 2 + 1 - c, x)
    pending = []

    def remote(src, dst, slot, device, recv_slot=None):
        return pltpu.make_async_remote_copy(
            src_ref=src, dst_ref=dst, send_sem=ss.at[slot],
            recv_sem=rs.at[slot if recv_slot is None else recv_slot],
            device_id=device, device_id_type=MESH,
        )

    def send(*args):
        copy = remote(*args)
        copy.start()
        pending.append(copy)
        return copy

    def block_of(i, n):
        return pl.ds(pl.multiple_of(i * n, n), n)

    def rows_of(dy, dz):
        return block_of(lax.rem(y + dy, CY) * CZ + lax.rem(z + dz, CZ), 8)

    mine, other = block_of(c, 256), block_of(1 - c, 256)
    half_cols = rows // 2
    halves = [pl.ds(0, half_cols), pl.ds(half_cols, half_cols)]

    loads = {}
    for i, (name, src, dst) in enumerate(
        (
            ("piv_s", pivots, piv_s),
            ("look", look, look_v),
            ("piv_v", piv_row, piv_v),
            ("panel", panel, gath.at[pl.ds(0, 64), :]),
            ("map", smap, sm_v),
            ("upper", upper, up_v),
            ("lower", lower, low_v),
        )
    ):
        loads[name] = pltpu.make_async_copy(src, dst, ld.at[i])
        loads[name].start()

    bar = pltpu.get_barrier_semaphore()

    def greet(device):
        pl.semaphore_signal(bar, inc=1, device_id=device, device_id_type=MESH)

    partners = [chip(d, 0) for d in range(1, CY)] + [chip(0, d) for d in range(1, CZ)]
    partners += [to_x(1), to_x(3), sibling]
    for device in partners:
        greet(device)

    @pl.when((y > 0) & (z > 0))
    def _():
        greet((c, x))

    @pl.when(r == 1)
    def _():
        for d in range(1, 4):
            greet((0, lax.rem(x + d, 4)))

    loads["piv_s"].wait()
    loads["look"].wait()

    def pick_rows(i, carry):
        pos = lax.rem(i, CZ)
        step = lax.div(pos + 1, 2)
        dz = jnp.where(lax.rem(pos, 2) == 1, 4 - step, 4 + step)
        start = (lax.div(i, CZ) * CZ + lax.rem(z + dz, CZ)) * 8
        for k in range(8):
            row = i * 8 + k
            local = piv_s[start + k] - first
            owned = (local >= 0) & (local < rows)
            at = jnp.where(owned, local, 0)
            pick[pl.ds(row, 1), :] = jnp.where(owned, look_v[pl.ds(at, 1), :], 0.0)
        return carry

    lax.fori_loop(0, NB // 8, pick_rows, 0)

    extra = (CY - 1) * (CZ - 1)

    @pl.when(r == 0)
    def _():
        pl.semaphore_wait(bar, len(partners) + extra + 3)

    @pl.when(r == 1)
    def _():
        pl.semaphore_wait(bar, len(partners) + extra)

    @pl.when(r > 1)
    def _():
        pl.semaphore_wait(bar, len(partners))

    a_core = []
    for d in (2, 1, 3, 0):
        block = block_of(lax.rem(y + d, CY), 64)
        a_core.append((d, block, send(pick.at[block, other], cbuf.at[block, :], A_CORE + d, sibling)))

    def share(ref, q):
        return ref.at[block_of(lax.rem(q, CY) * CZ + lax.div(q, CY), 8), :]

    def shares(src, dst, act):
        def one(q, carry):
            act(remote(share(src, q), share(dst, q), H_S + q, (2 * q + c, x), H_R))
            return carry

        lax.fori_loop(1, CHIPS, one, 0)

    def columns(to):
        return remote(panel.at[:, pl.ds(0, NB)], deal.at[block_of(x, 64), :], H_X + to, (1, to), H_X + x)

    own_head = pltpu.make_async_copy(look.at[pl.ds(0, 8), :], head.at[pl.ds(0, 8), :], ld.at[7])

    @pl.when(r == 0)
    def _():
        for to in range(4):
            columns(to).start()
        own_head.start()
        shares(look, head, lambda copy: copy.start())

    right, left = to_x(1), to_x(3)
    ring = [
        send(panel.at[:, halves[0]], gath.at[pl.ds(128, 64), halves[0]], X_RING, right),
        send(panel.at[:, halves[1]], gath.at[pl.ds(64, 64), halves[1]], X_RING + 2, left),
        send(panel.at[:, halves[1]], gath.at[pl.ds(128, 64), halves[1]], X_RING + 1, right),
        send(panel.at[:, halves[0]], gath.at[pl.ds(64, 64), halves[0]], X_RING + 3, left),
    ]

    def group(block, g):
        return hsum.at[pl.ds(pl.multiple_of(block * 64 + g * 32, 32), 32), :]

    a_y = {}
    for d, block, copy in a_core:
        copy.wait_recv()
        hsum[block, :] = pick[block, mine] + cbuf[block, :]
        if d:
            part = group(lax.rem(y + d, CY), 0)
            a_y[d, 0] = send(part, ybuf.at[d - 1, pl.ds(0, 32), :], A_Y + d, chip(d, 0))
    for d in (2, 1, 3):
        part = group(lax.rem(y + d, CY), 1)
        a_y[d, 1] = send(part, ybuf.at[d - 1, pl.ds(32, 32), :], A_Y + 4 + d, chip(d, 0))

    @pl.when(r == 1)
    def _():
        for q in range(4):
            block = deal.at[pl.ds(64 * q, 64), :]
            remote(block, block, H_X + q, sibling).wait_recv()
        phead[pl.ds(0, 8), :] = deal[pl.ds(0, 8), :]
        shares(deal, phead, lambda copy: copy.start())

    loads["panel"].wait()
    loads["piv_v"].wait()
    loads["map"].wait()
    spart[...] = jnp.zeros_like(spart)
    tile = 256
    wide = jnp.broadcast_to(piv_v[...], (NB, NB))
    tall = wide.T

    def small(i, carry):
        cols = block_of(i, tile)
        p = gath[0:64, cols]
        p1, p2 = split(p)
        p3 = (p - p1.astype(F32) - p2.astype(F32)).astype(BF16)
        mh, ml = split(sm_v[:, cols])
        nt = ((1,), (1,))
        both = dot(jnp.concatenate([p1, p2], 0), mh, nt)
        spart[0:64, :] += both[0:64] + both[64:128] + dot(p1, ml, nt)
        start = first + i * tile
        at = lax.broadcasted_iota(jnp.int32, (tile, NB), 0) + start
        hot = jnp.where(at == wide, 1.0, 0.0).astype(BF16)
        left_ref[cols, 512:768] = hot
        at = lax.broadcasted_iota(jnp.int32, (NB, tile), 1) + start
        turned = jnp.where(at == tall, 1.0, 0.0)
        hot_t[:, cols] = turned.astype(BF16)
        hit[:, cols] = jnp.broadcast_to(jnp.max(turned, axis=0, keepdims=True), (8, tile))
        three = dot(jnp.concatenate([p1, p2, p3], 0), hot)
        spart[64:128, :] += three[0:64] + three[64:128] + three[128:192]
        return carry

    lax.fori_loop(0, rows // tile, small, 0, unroll=8)
    s_core = send(spart.at[block_of(1 - c, 64), :], scbuf, S_CORE, sibling)

    order = [block_of(lax.rem(x + d, 4), 64) for d in (0, 1, 3, 2)]

    def reorder(ref):
        return jnp.concatenate([ref[block, :] for block in order], 0)

    loads["upper"].wait()
    loads["lower"].wait()
    i = lax.broadcasted_iota(jnp.int32, (NB, NB), 0)
    j = lax.broadcasted_iota(jnp.int32, (NB, NB), 1)
    low = split(jnp.where(i > j, low_v[...], jnp.where(i == j, 1.0, 0.0)))
    up_v[...] = jnp.where(i <= j, up_v[...], 0.0)
    up = reorder(up_v)
    lowh[...], lowl[...] = low
    mulh[...], mull[...] = split(dot3(split(up), low))
    up_v[...] = up.T
    u = split(up_v[block_of(x, 64), :])
    both_u[...] = jnp.concatenate(u, 0)

    s_core.wait_recv()
    ssum[...] = spart[block_of(c, 64), :] + scbuf[...]
    s_y = [send(ssum.at[block_of(lax.rem(y + d, CY), 16), :], sybuf.at[d - 1], S_Y + d, chip(d, 0)) for d in range(1, CY)]

    a_z = []
    for g in range(2):
        for d in range(1, CY):
            a_y[d, g].wait_recv()
        part = pl.ds(32 * g, 32)
        zin[part, :] = hsum[pl.ds(pl.multiple_of(y * 64 + 32 * g, 32), 32), :] + ybuf[0, part, :] + ybuf[1, part, :] + ybuf[2, part, :]
        for pos in range(4 * g, 4 * g + 4):
            d = (FAR_Z + (0,))[pos]
            if d:
                a_z.append(send(zin.at[pl.ds(8 * pos, 8), :], zbuf.at[d - 1], A_Z + d, chip(0, d)))

    own = rows_of(0, 0)

    def by_core(stage):
        pl.when(c == 0)(lambda: stage(head))
        pl.when(c == 1)(lambda: stage(phead))

    def over_z(buf, d):
        return remote(buf.at[own, :], buf.at[own, :], H_GZ + d, chip(0, d))

    def over_y(buf, d, e):
        part = buf.at[rows_of(0, CZ - e), :]
        return remote(part, part, H_GY + d * CZ + e, chip(d, 0))

    def over_core(buf, d):
        part = buf.at[block_of(lax.rem(y + d, CY), 64), :]
        return remote(part, part, H_GC + d, sibling)

    def head_over_z(buf):
        @pl.when(r > 1)
        def _():
            remote(buf.at[own, :], buf.at[own, :], H_R, sibling).wait_recv()

        for d in FAR_Z:
            over_z(buf, d).start()
        for d in range(1, CY):
            over_y(buf, d, 0).start()

    def head_over_y(buf):
        for e in NEAR_Z:
            over_z(buf, e).wait_recv()
            for d in (2, 1, 3):
                over_y(buf, d, e).start()
        over_core(buf, 0).start()

    def head_over_core(buf):
        for d in (1, 3, 2):
            for e in range(CZ):
                over_y(buf, CY - d, e).wait_recv()
            over_core(buf, d).start()

    def head_arrived(buf):
        for d in range(CY):
            over_core(buf, d).wait_recv()

    def head_left(buf):
        for d in range(1, CZ):
            over_z(buf, d).wait_send()
        for d in range(1, CY):
            for e in range(CZ):
                over_y(buf, d, e).wait_send()
        for d in range(CY):
            over_core(buf, d).wait_send()

    pl.when(r == 0)(own_head.wait)
    by_core(head_over_z)

    for copy in s_y:
        copy.wait_recv()
    szbuf[z] = ssum[block_of(y, 16), :] + sybuf[0] + sybuf[1] + sybuf[2]

    def small_over_z(d):
        return remote(szbuf.at[z], szbuf.at[z], S_Z + d, chip(0, d))

    def small_to_root():
        return remote(szbuf.at[z], szbuf.at[z], S_Z + lax.rem(CZ - z, CZ), (2 * y + 1, x))

    @pl.when(c == 0)
    def _():
        for d in FAR_Z:
            small_over_z(d).start()

    @pl.when((c == 1) & (z > 0))
    def _():
        small_to_root().start()

    far = pl.ds(192, 64)
    ring[0].wait_recv()
    ring.append(send(gath.at[pl.ds(128, 64), halves[0]], gath.at[far, halves[0]], X_RING + 4, right))
    ring[1].wait_recv()
    ring.append(send(gath.at[pl.ds(64, 64), halves[1]], gath.at[far, halves[1]], X_RING + 5, left))

    for copy in a_z:
        copy.wait_recv()
    total = zin[56:64, :]
    for d in range(1, CZ):
        total = total + zbuf[d - 1]
    piv[own, mine] = total
    a_gz = {d: send(piv.at[own, mine], piv.at[own, mine], A_GZ + d, chip(0, d)) for d in FAR_Z}
    a_gy = {}

    def a_over_y(e):
        part = piv.at[rows_of(0, CZ - e), mine]
        for d in (2, 1, 3):
            a_gy[d, e] = send(part, part, A_GY + d * CZ + e, chip(d, 0))

    a_over_y(0)

    def turn_half(g):
        span = pl.ds(128 * g, 128)
        for copy in (ring[3],) if g == 0 else (ring[2], ring[4], ring[5]):
            copy.wait_recv()

        def turn(i, carry):
            at = block_of(i, 256)
            kept = jnp.where(hit[0:1, at] > 0.0, 0.0, gath[span, at])
            hi, lo = split(kept)
            pre = dot(both_u[:, span], hi)
            pre = pre[0:64] + pre[64:128] + dot(both_u[0:64, span], lo)
            lp[:, at] = pre if g == 0 else lp[:, at] + pre
            left_ref[at, span] = lo.T
            left_ref[at, pl.ds(256 + 128 * g, 128)] = hi.T
            return carry

        lax.fori_loop(0, rows // 256, turn, 0, unroll=8)

    by_core(head_over_y)
    for e in NEAR_Z[:4]:
        a_gz[e].wait_recv()
        a_over_y(e)

    at_small = block_of(c * CY + y, 16)

    def small_over_y(d):
        return remote(red.at[at_small, :], red.at[at_small, :], S_GY + d, chip(d, 0))

    def small_to_root_y():
        return remote(red.at[at_small, :], red.at[at_small, :], S_GY + lax.rem(CY - y, CY), (1, x))

    def small_to_core():
        part = red.at[block_of(c, 64), :]
        return remote(part, part, S_GC, sibling)

    @pl.when((c == 0) | (z == 0))
    def _():
        for d in range(1, CZ):
            small_over_z(d).wait_recv()
        total = szbuf[0]
        for q in range(1, CZ):
            total = total + szbuf[q]
        red[at_small, :] = total

    @pl.when(c == 0)
    def _():
        for d in range(1, CY):
            small_over_y(d).start()

    @pl.when((c == 1) & (z == 0) & (y > 0))
    def _():
        small_to_root_y().start()

    turn_half(0)
    for e in NEAR_Z[4:]:
        a_gz[e].wait_recv()
        a_over_y(e)
    a_gc = []
    for d in (0, 1, 3, 2):
        for e in range(CZ):
            if d:
                a_gy[CY - d, e].wait_recv()
        part = piv.at[block_of(lax.rem(y + d, CY), 64), mine]
        a_gc.append(send(part, part, A_GC + d, sibling))

    by_core(head_over_core)

    @pl.when((c == 0) | (r == 1))
    def _():
        for d in range(1, CY):
            small_over_y(d).wait_recv()
        small_to_core().start()

    for copy in a_gc:
        copy.wait_recv()
    rows_in = split(piv[...])
    vh, vl = split(dot3((mulh[...], mull[...]), rows_in))
    va[0:256, :] = -vh
    va[256:512, :] = -vh
    vb[0:256, :] = -vl

    @pl.when(r == 0)
    def _():
        ur[...] = dot3((lowh[...], lowl[...]), rows_in)

    turn_half(1)

    pl.when(c == 0)(lambda: head_arrived(phead))
    pl.when(c == 1)(lambda: head_arrived(head))
    cols = reorder(phead)
    moved = (head[...] - piv[...]) - dot3(split(cols.T), (vh, vl))
    dh, dl = split(moved)
    va[512:768, :] = dh
    vb[256:512, :] = dl
    both_f = jnp.concatenate(split(dot3((both_u[0:64, :], both_u[64:128, :]), split(cols))), 0)

    add = dot(both_f, hot_t[...])
    lp[...] += add[0:64] + add[64:128]

    @pl.when((c == 1) | (r == 0))
    def _():
        small_to_core().wait_recv()

    sk[...] = red[0:64, :]

    @pl.when(r == 0)
    def _():
        lp[:, 0:NB] = red[64:128, :]

    for copy in pending:
        copy.wait_send()
    by_core(head_left)

    @pl.when(c == 0)
    def _():
        for d in range(1, CZ):
            small_over_z(d).wait_send()
        for d in range(1, CY):
            small_over_y(d).wait_send()

    @pl.when((c == 1) & (z > 0))
    def _():
        small_to_root().wait_send()

    @pl.when((c == 1) & (z == 0) & (y > 0))
    def _():
        small_to_root_y().wait_send()

    @pl.when((c == 0) | (r == 1))
    def _():
        small_to_core().wait_send()

    @pl.when(r == 0)
    def _():
        for to in range(4):
            columns(to).wait_send()
        shares(look, head, lambda copy: copy.wait_send())

    @pl.when(r == 1)
    def _():
        shares(deal, phead, lambda copy: copy.wait_send())


def update_kernel(first, look, left_ref, va, vb, ur, lp, sk, out, lp_out, sk_out, buf, sem, small_sem):
    tile = buf.shape[1]
    steps = buf.shape[0]
    small = [
        pltpu.make_async_copy(lp, lp_out, small_sem.at[0]),
        pltpu.make_async_copy(sk, sk_out, small_sem.at[1]),
    ]
    for copy in small:
        copy.start()

    def block(i):
        return pl.ds(pl.multiple_of(i * tile, tile), tile)

    def write(i):
        return pltpu.make_async_copy(buf.at[i], out.at[block(i), :], sem.at[i])

    def step(i, carry):
        at = block(i)
        buf[i] = look[at, :] + dot(left_ref[at, :], va[...]) + dot(left_ref[at, 256:768], vb[...])

        @pl.when((i == 0) & (first[0] == 0))
        def _():
            buf[0, 0:NB, :] = ur[...]

        write(i).start()
        return carry

    lax.fori_loop(0, steps, step, 0, unroll=True)
    for copy in small:
        copy.wait()
    for i in range(steps):
        write(i).wait()


def on_device(panel_col, look_cols, sketch_map, upper_inv, lower_inv, pivots):
    rows, width = look_cols.shape
    panel_t = panel_col.T
    piv_row = pivots.reshape(1, NB)
    vmem = pl.BlockSpec(memory_space=pltpu.VMEM)
    hbm = pl.BlockSpec(memory_space=pltpu.HBM)
    inputs = [
        pltpu.with_memory_space_constraint(a, pltpu.HBM)
        for a in (pivots, piv_row, panel_t, look_cols, sketch_map, upper_inv, lower_inv)
    ]
    results = pl.pallas_call(
        exchange_kernel,
        out_shape=(
            jax.ShapeDtypeStruct((rows, 3 * NB), BF16),
            jax.ShapeDtypeStruct((3 * NB, width), BF16),
            jax.ShapeDtypeStruct((2 * NB, width), BF16),
            jax.ShapeDtypeStruct((NB, width), F32),
            jax.ShapeDtypeStruct((64, rows), F32),
            jax.ShapeDtypeStruct((64, NB), F32),
        ),
        in_specs=[hbm] * len(inputs),
        out_specs=(vmem,) * 6,
        scratch_shapes=[
            pltpu.SMEM((NB,), jnp.int32),
            pltpu.VMEM((1, NB), jnp.int32),
            pltpu.VMEM((rows, width), F32),
            pltpu.VMEM((NB, rows), F32),
            pltpu.VMEM((NB, NB), F32),
            pltpu.VMEM((NB, NB), F32),
            pltpu.VMEM((NB, rows), F32),
            pltpu.VMEM((NB, rows), BF16),
            pltpu.VMEM((8, rows), F32),
            pltpu.VMEM((NB, width), F32),
            pltpu.VMEM((NB, 256), F32),
            pltpu.VMEM((NB, 256), F32),
            pltpu.VMEM((3, 64, 256), F32),
            pltpu.VMEM((64, 256), F32),
            pltpu.VMEM((7, 8, 256), F32),
            pltpu.VMEM((NB, width), F32),
            pltpu.VMEM((NB, width), F32),
            pltpu.VMEM((NB, NB), F32),
            pltpu.VMEM((NB, NB), F32),
            pltpu.VMEM((128, NB), F32),
            pltpu.VMEM((64, NB), F32),
            pltpu.VMEM((64, NB), F32),
            pltpu.VMEM((3, 16, NB), F32),
            pltpu.VMEM((CZ, 16, NB), F32),
            pltpu.VMEM((128, NB), F32),
            pltpu.VMEM((NB, NB), BF16),
            pltpu.VMEM((NB, NB), BF16),
            pltpu.VMEM((NB, NB), BF16),
            pltpu.VMEM((NB, NB), BF16),
            pltpu.VMEM((128, NB), BF16),
            pltpu.SemaphoreType.DMA((8,)),
            pltpu.SemaphoreType.DMA((N_SEM,)),
            pltpu.SemaphoreType.DMA((N_SEM,)),
        ],
        compiler_params=pltpu.CompilerParams(
            collective_id=0, has_side_effects=True, vmem_limit_bytes=36 << 20
        ),
        name="exchange",
    )(*inputs)

    first = (lax.axis_index("row") * rows).astype(jnp.int32).reshape(1)
    tile = 256
    updated, lp, sk = pl.pallas_call(
        update_kernel,
        out_shape=(
            jax.ShapeDtypeStruct((rows, width), F32),
            jax.ShapeDtypeStruct((64, rows), F32),
            jax.ShapeDtypeStruct((64, NB), F32),
        ),
        in_specs=[pl.BlockSpec(memory_space=pltpu.SMEM)] + [vmem] * 7,
        out_specs=(hbm,) * 3,
        scratch_shapes=[
            pltpu.VMEM((rows // tile, tile, width), F32),
            pltpu.SemaphoreType.DMA((rows // tile,)),
            pltpu.SemaphoreType.DMA((2,)),
        ],
        compiler_params=pltpu.CompilerParams(vmem_limit_bytes=32 << 20),
        name="update",
    )(first, look_cols, *results)
    return lp.T, updated, sk.T


def solution(mesh):
    placed = (P("row", "col"), P("row", "col"), P(None, "row"), P(), P(), P())
    return jax.shard_map(
        on_device,
        mesh=mesh,
        in_specs=placed,
        out_specs=(P("row", "col"), P("row", "col"), P(None, "col")),
        check_vma=False,
    )
```

```python
import jax
import jax.numpy as jnp
from jax import lax
from jax.experimental import pallas as pl
from jax.experimental.pallas import tpu as pltpu
from jax.sharding import PartitionSpec as P

MESH = pl.DeviceIdType.MESH
F32, BF16 = jnp.float32, jnp.bfloat16
NB = 256
CY, CZ = 4, 8
CHIPS = CY * CZ

X_RING = 0
A_CORE = 6
A_Y = 10
A_Z = 18
A_GZ = 26
A_GY = 42
A_GC = 74
S_CORE = 78
S_Y = 79
S_Z = 83
S_GY = 91
S_GC = 95
H_X = 96
H_S = 100
H_R = 132
H_GZ = 133
H_GY = 141
H_GC = 173
N_SEM = 177

FAR_Z = (4, 3, 5, 2, 6, 1, 7)
NEAR_Z = (1, 7, 2, 6, 3, 5, 4)


def split(a):
    hi = a.astype(BF16)
    return hi, (a - hi.astype(F32)).astype(BF16)


def dot(a, b, dims=((1,), (0,))):
    return lax.dot_general(a, b, (dims, ((), ())), preferred_element_type=F32)


def dot3(a, b):
    (ah, al), (bh, bl) = a, b
    return dot(ah, bh) + dot(al, bh) + dot(ah, bl)


def exchange_kernel(
    pivots, piv_row, panel, look, smap, upper, lower,
    left_ref, va, vb, ur, lp, sk,
    piv_s, piv_v, look_a, look_b, sm_v, up_v, low_v, gath, hot_t, hit,
    pick, cbuf, hsum, ybuf, zin, zbuf, piv, head, phead, deal,
    spart, scbuf, ssum, sybuf, szbuf, red, lowh, lowl, mulh, mull, both_u,
    ld, ss, rs,
):
    r, x = lax.axis_index("row"), lax.axis_index("col")
    c = lax.rem(r, 2)
    y = lax.rem(lax.div(r, 2), CY)
    z = lax.div(r, 2 * CY)
    rows = look.shape[0]
    first = r * rows

    def chip(dy, dz):
        return ((lax.rem(z + dz, CZ) * CY + lax.rem(y + dy, CY)) * 2 + c, x)

    def to_x(d):
        return (r, lax.rem(x + d + 4, 4))

    sibling = ((z * CY + y) * 2 + 1 - c, x)
    pending = []

    def remote(src, dst, slot, device, recv_slot=None):
        return pltpu.make_async_remote_copy(
            src_ref=src, dst_ref=dst, send_sem=ss.at[slot],
            recv_sem=rs.at[slot if recv_slot is None else recv_slot],
            device_id=device, device_id_type=MESH,
        )

    def send(*args):
        copy = remote(*args)
        copy.start()
        pending.append(copy)
        return copy

    def block_of(i, n):
        return pl.ds(pl.multiple_of(i * n, n), n)

    def rows_of(dy, dz):
        return block_of(lax.rem(y + dy, CY) * CZ + lax.rem(z + dz, CZ), 8)

    mine, other = block_of(c, 256), block_of(1 - c, 256)
    half_cols = rows // 2
    halves = [pl.ds(0, half_cols), pl.ds(half_cols, half_cols)]

    loads = {}

    def load(name, src, dst):
        loads[name] = pltpu.make_async_copy(src, dst, ld.at[len(loads)])
        loads[name].start()

    load("piv_s", pivots, piv_s)
    load("other", look.at[:, other], look_a)
    load("mine", look.at[:, mine], look_b)
    load("piv_v", piv_row, piv_v)
    load("panel", panel, gath.at[pl.ds(0, 64), :])

    bar = pltpu.get_barrier_semaphore()

    def greet(device):
        pl.semaphore_signal(bar, inc=1, device_id=device, device_id_type=MESH)

    partners = [chip(d, 0) for d in range(1, CY)] + [chip(0, d) for d in range(1, CZ)]
    partners += [to_x(1), to_x(3), sibling]
    for device in partners:
        greet(device)

    @pl.when((y > 0) & (z > 0))
    def _():
        greet((c, x))

    @pl.when(r == 1)
    def _():
        for d in range(1, 4):
            greet((0, lax.rem(x + d, 4)))

    loads["piv_s"].wait()

    def pick_half(half, look_v):
        def pick_rows(i, carry):
            pos = lax.rem(i, CZ)
            step = lax.div(pos + 1, 2)
            dz = jnp.where(lax.rem(pos, 2) == 1, 4 - step, 4 + step)
            start = (lax.div(i, CZ) * CZ + lax.rem(z + dz, CZ)) * 8
            for k in range(8):
                local = piv_s[start + k] - first
                owned = (local >= 0) & (local < rows)
                at = jnp.where(owned, local, 0)
                pick[half, pl.ds(i * 8 + k, 1), :] = jnp.where(owned, look_v[pl.ds(at, 1), :], 0.0)
            return carry

        lax.fori_loop(0, NB // 8, pick_rows, 0, unroll=1)

    loads["other"].wait()
    pick_half(0, look_a)
    extra = (CY - 1) * (CZ - 1)

    @pl.when(r == 0)
    def _():
        pl.semaphore_wait(bar, len(partners) + extra + 3)

    @pl.when(r == 1)
    def _():
        pl.semaphore_wait(bar, len(partners) + extra)

    @pl.when(r > 1)
    def _():
        pl.semaphore_wait(bar, len(partners))

    a_core = []
    for d in (2, 1, 3, 0):
        block = block_of(lax.rem(y + d, CY), 64)
        a_core.append((d, block, send(pick.at[0, block, :], cbuf.at[block, :], A_CORE + d, sibling)))

    def share(ref, q):
        return ref.at[block_of(lax.rem(q, CY) * CZ + lax.div(q, CY), 8), :]

    def shares(src, dst, act):
        def one(q, carry):
            act(remote(share(src, q), share(dst, q), H_S + q, (2 * q + c, x), H_R))
            return carry

        lax.fori_loop(1, CHIPS, one, 0)

    def columns(to):
        return remote(panel.at[:, pl.ds(0, NB)], deal.at[block_of(x, 64), :], H_X + to, (1, to), H_X + x)

    own_head = pltpu.make_async_copy(look.at[pl.ds(0, 8), :], head.at[pl.ds(0, 8), :], ld.at[8])

    @pl.when(r == 0)
    def _():
        for to in range(4):
            columns(to).start()
        own_head.start()
        shares(look, head, lambda copy: copy.start())

    right, left = to_x(1), to_x(3)
    ring = [
        send(panel.at[:, halves[0]], gath.at[pl.ds(128, 64), halves[0]], X_RING, right),
        send(panel.at[:, halves[1]], gath.at[pl.ds(64, 64), halves[1]], X_RING + 2, left),
        send(panel.at[:, halves[1]], gath.at[pl.ds(128, 64), halves[1]], X_RING + 1, right),
        send(panel.at[:, halves[0]], gath.at[pl.ds(64, 64), halves[0]], X_RING + 3, left),
    ]

    load("map", smap, sm_v)
    load("upper", upper, up_v)
    load("lower", lower, low_v)
    loads["mine"].wait()
    pick_half(1, look_b)

    def group(block, g):
        return hsum.at[pl.ds(pl.multiple_of(block * 64 + g * 32, 32), 32), :]

    a_y = {}
    for d, block, copy in a_core:
        copy.wait_recv()
        hsum[block, :] = pick[1, block, :] + cbuf[block, :]
        if d:
            part = group(lax.rem(y + d, CY), 0)
            a_y[d, 0] = send(part, ybuf.at[d - 1, pl.ds(0, 32), :], A_Y + d, chip(d, 0))
    for d in (2, 1, 3):
        part = group(lax.rem(y + d, CY), 1)
        a_y[d, 1] = send(part, ybuf.at[d - 1, pl.ds(32, 32), :], A_Y + 4 + d, chip(d, 0))

    @pl.when(r == 1)
    def _():
        for q in range(4):
            block = deal.at[pl.ds(64 * q, 64), :]
            remote(block, block, H_X + q, sibling).wait_recv()
        phead[pl.ds(0, 8), :] = deal[pl.ds(0, 8), :]
        shares(deal, phead, lambda copy: copy.start())

    loads["panel"].wait()
    loads["piv_v"].wait()
    loads["map"].wait()
    spart[...] = jnp.zeros_like(spart)
    tile = 256
    wide = jnp.broadcast_to(piv_v[...], (NB, NB))
    tall = wide.T

    def small(i, carry):
        cols = block_of(i, tile)
        p = gath[0:64, cols]
        p1, p2 = split(p)
        p3 = (p - p1.astype(F32) - p2.astype(F32)).astype(BF16)
        mh, ml = split(sm_v[:, cols])
        nt = ((1,), (1,))
        both = dot(jnp.concatenate([p1, p2], 0), mh, nt)
        spart[0:64, :] += both[0:64] + both[64:128] + dot(p1, ml, nt)
        start = first + i * tile
        at = lax.broadcasted_iota(jnp.int32, (tile, NB), 0) + start
        hot = jnp.where(at == wide, 1.0, 0.0).astype(BF16)
        left_ref[cols, 512:768] = hot
        at = lax.broadcasted_iota(jnp.int32, (NB, tile), 1) + start
        turned = jnp.where(at == tall, 1.0, 0.0)
        hot_t[:, cols] = turned.astype(BF16)
        hit[:, cols] = jnp.broadcast_to(jnp.max(turned, axis=0, keepdims=True), (8, tile))
        three = dot(jnp.concatenate([p1, p2, p3], 0), hot)
        spart[64:128, :] += three[0:64] + three[64:128] + three[128:192]
        return carry

    lax.fori_loop(0, rows // tile, small, 0, unroll=8)
    s_core = send(spart.at[block_of(1 - c, 64), :], scbuf, S_CORE, sibling)

    order = [block_of(lax.rem(x + d, 4), 64) for d in (0, 1, 3, 2)]

    def reorder(ref):
        return jnp.concatenate([ref[block, :] for block in order], 0)

    loads["upper"].wait()
    loads["lower"].wait()
    i = lax.broadcasted_iota(jnp.int32, (NB, NB), 0)
    j = lax.broadcasted_iota(jnp.int32, (NB, NB), 1)
    low = split(jnp.where(i > j, low_v[...], jnp.where(i == j, 1.0, 0.0)))
    up_v[...] = jnp.where(i <= j, up_v[...], 0.0)
    up = reorder(up_v)
    lowh[...], lowl[...] = low
    mulh[...], mull[...] = split(dot3(split(up), low))
    up_v[...] = up.T
    u = split(up_v[block_of(x, 64), :])
    both_u[...] = jnp.concatenate(u, 0)

    s_core.wait_recv()
    ssum[...] = spart[block_of(c, 64), :] + scbuf[...]
    s_y = [send(ssum.at[block_of(lax.rem(y + d, CY), 16), :], sybuf.at[d - 1], S_Y + d, chip(d, 0)) for d in range(1, CY)]

    a_z = []
    for g in range(2):
        for d in range(1, CY):
            a_y[d, g].wait_recv()
        part = pl.ds(32 * g, 32)
        zin[part, :] = hsum[pl.ds(pl.multiple_of(y * 64 + 32 * g, 32), 32), :] + ybuf[0, part, :] + ybuf[1, part, :] + ybuf[2, part, :]
        for pos in range(4 * g, 4 * g + 4):
            d = (FAR_Z + (0,))[pos]
            if d:
                a_z.append(send(zin.at[pl.ds(8 * pos, 8), :], zbuf.at[d - 1], A_Z + d, chip(0, d)))

    own = rows_of(0, 0)

    def by_core(stage):
        pl.when(c == 0)(lambda: stage(head))
        pl.when(c == 1)(lambda: stage(phead))

    def over_z(buf, d):
        return remote(buf.at[own, :], buf.at[own, :], H_GZ + d, chip(0, d))

    def over_y(buf, d, e):
        part = buf.at[rows_of(0, CZ - e), :]
        return remote(part, part, H_GY + d * CZ + e, chip(d, 0))

    def over_core(buf, d):
        part = buf.at[block_of(lax.rem(y + d, CY), 64), :]
        return remote(part, part, H_GC + d, sibling)

    def head_over_z(buf):
        @pl.when(r > 1)
        def _():
            remote(buf.at[own, :], buf.at[own, :], H_R, sibling).wait_recv()

        for d in FAR_Z:
            over_z(buf, d).start()
        for d in range(1, CY):
            over_y(buf, d, 0).start()

    def head_over_y(buf):
        for e in NEAR_Z:
            over_z(buf, e).wait_recv()
            for d in (2, 1, 3):
                over_y(buf, d, e).start()
        over_core(buf, 0).start()

    def head_over_core(buf):
        for d in (1, 3, 2):
            for e in range(CZ):
                over_y(buf, CY - d, e).wait_recv()
            over_core(buf, d).start()

    def head_arrived(buf):
        for d in range(CY):
            over_core(buf, d).wait_recv()

    def head_left(buf):
        for d in range(1, CZ):
            over_z(buf, d).wait_send()
        for d in range(1, CY):
            for e in range(CZ):
                over_y(buf, d, e).wait_send()
        for d in range(CY):
            over_core(buf, d).wait_send()

    pl.when(r == 0)(own_head.wait)
    by_core(head_over_z)

    for copy in s_y:
        copy.wait_recv()
    szbuf[z] = ssum[block_of(y, 16), :] + sybuf[0] + sybuf[1] + sybuf[2]

    def small_over_z(d):
        return remote(szbuf.at[z], szbuf.at[z], S_Z + d, chip(0, d))

    def small_to_root():
        return remote(szbuf.at[z], szbuf.at[z], S_Z + lax.rem(CZ - z, CZ), (2 * y + 1, x))

    @pl.when(c == 0)
    def _():
        for d in FAR_Z:
            small_over_z(d).start()

    @pl.when((c == 1) & (z > 0))
    def _():
        small_to_root().start()

    for copy in a_z:
        copy.wait_recv()
    total = zin[56:64, :]
    for d in range(1, CZ):
        total = total + zbuf[d - 1]
    piv[own, mine] = total
    a_gz = {d: send(piv.at[own, mine], piv.at[own, mine], A_GZ + d, chip(0, d)) for d in FAR_Z}
    a_gy = {}

    def a_over_y(e):
        part = piv.at[rows_of(0, CZ - e), mine]
        for d in (2, 1, 3):
            a_gy[d, e] = send(part, part, A_GY + d * CZ + e, chip(d, 0))

    a_over_y(0)

    far = pl.ds(192, 64)
    ring[0].wait_recv()
    ring.append(send(gath.at[pl.ds(128, 64), halves[0]], gath.at[far, halves[0]], X_RING + 4, right))
    ring[1].wait_recv()
    ring.append(send(gath.at[pl.ds(64, 64), halves[1]], gath.at[far, halves[1]], X_RING + 5, left))


    def turn_half(g):
        span = pl.ds(128 * g, 128)
        for copy in (ring[3],) if g == 0 else (ring[2], ring[4], ring[5]):
            copy.wait_recv()

        def turn(i, carry):
            at = block_of(i, 256)
            kept = jnp.where(hit[0:1, at] > 0.0, 0.0, gath[span, at])
            hi, lo = split(kept)
            pre = dot(both_u[:, span], hi)
            pre = pre[0:64] + pre[64:128] + dot(both_u[0:64, span], lo)
            lp[:, at] = pre if g == 0 else lp[:, at] + pre
            left_ref[at, span] = lo.T
            left_ref[at, pl.ds(256 + 128 * g, 128)] = hi.T
            return carry

        lax.fori_loop(0, rows // 256, turn, 0, unroll=8)

    by_core(head_over_y)
    for e in NEAR_Z[:4]:
        a_gz[e].wait_recv()
        a_over_y(e)

    at_small = block_of(c * CY + y, 16)

    def small_over_y(d):
        return remote(red.at[at_small, :], red.at[at_small, :], S_GY + d, chip(d, 0))

    def small_to_root_y():
        return remote(red.at[at_small, :], red.at[at_small, :], S_GY + lax.rem(CY - y, CY), (1, x))

    def small_to_core():
        part = red.at[block_of(c, 64), :]
        return remote(part, part, S_GC, sibling)

    @pl.when((c == 0) | (z == 0))
    def _():
        for d in range(1, CZ):
            small_over_z(d).wait_recv()
        total = szbuf[0]
        for q in range(1, CZ):
            total = total + szbuf[q]
        red[at_small, :] = total

    @pl.when(c == 0)
    def _():
        for d in range(1, CY):
            small_over_y(d).start()

    @pl.when((c == 1) & (z == 0) & (y > 0))
    def _():
        small_to_root_y().start()

    turn_half(0)
    for e in NEAR_Z[4:]:
        a_gz[e].wait_recv()
        a_over_y(e)
    a_gc = []
    for d in (0, 1, 3, 2):
        for e in range(CZ):
            if d:
                a_gy[CY - d, e].wait_recv()
        part = piv.at[block_of(lax.rem(y + d, CY), 64), mine]
        a_gc.append(send(part, part, A_GC + d, sibling))

    by_core(head_over_core)

    @pl.when((c == 0) | (r == 1))
    def _():
        for d in range(1, CY):
            small_over_y(d).wait_recv()
        small_to_core().start()

    for copy in a_gc:
        copy.wait_recv()
    rows_in = split(piv[...])
    vh, vl = split(dot3((mulh[...], mull[...]), rows_in))
    va[0:256, :] = -vh
    va[256:512, :] = -vh
    vb[0:256, :] = -vl

    @pl.when(r == 0)
    def _():
        ur[...] = dot3((lowh[...], lowl[...]), rows_in)

    turn_half(1)

    pl.when(c == 0)(lambda: head_arrived(phead))
    pl.when(c == 1)(lambda: head_arrived(head))
    cols = reorder(phead)
    moved = (head[...] - piv[...]) - dot3(split(cols.T), (vh, vl))
    dh, dl = split(moved)
    va[512:768, :] = dh
    vb[256:512, :] = dl
    both_f = jnp.concatenate(split(dot3((both_u[0:64, :], both_u[64:128, :]), split(cols))), 0)

    add = dot(both_f, hot_t[...])
    lp[...] += add[0:64] + add[64:128]

    @pl.when((c == 1) | (r == 0))
    def _():
        small_to_core().wait_recv()

    sk[...] = red[0:64, :]

    @pl.when(r == 0)
    def _():
        lp[:, 0:NB] = red[64:128, :]

    for copy in pending:
        copy.wait_send()
    by_core(head_left)

    @pl.when(c == 0)
    def _():
        for d in range(1, CZ):
            small_over_z(d).wait_send()
        for d in range(1, CY):
            small_over_y(d).wait_send()

    @pl.when((c == 1) & (z > 0))
    def _():
        small_to_root().wait_send()

    @pl.when((c == 1) & (z == 0) & (y > 0))
    def _():
        small_to_root_y().wait_send()

    @pl.when((c == 0) | (r == 1))
    def _():
        small_to_core().wait_send()

    @pl.when(r == 0)
    def _():
        for to in range(4):
            columns(to).wait_send()
        shares(look, head, lambda copy: copy.wait_send())

    @pl.when(r == 1)
    def _():
        shares(deal, phead, lambda copy: copy.wait_send())


def update_kernel(first, look, left_ref, va, vb, ur, lp, sk, out, lp_out, sk_out, buf, sem, small_sem):
    tile = buf.shape[1]
    steps = buf.shape[0]
    small = [
        pltpu.make_async_copy(lp, lp_out, small_sem.at[0]),
        pltpu.make_async_copy(sk, sk_out, small_sem.at[1]),
    ]
    for copy in small:
        copy.start()

    def block(i):
        return pl.ds(pl.multiple_of(i * tile, tile), tile)

    def write(i):
        return pltpu.make_async_copy(buf.at[i], out.at[block(i), :], sem.at[i])

    def step(i, carry):
        at = block(i)
        buf[i] = look[at, :] + dot(left_ref[at, :], va[...]) + dot(left_ref[at, 256:768], vb[...])

        @pl.when((i == 0) & (first[0] == 0))
        def _():
            buf[0, 0:NB, :] = ur[...]

        write(i).start()
        return carry

    lax.fori_loop(0, steps, step, 0, unroll=True)
    for copy in small:
        copy.wait()
    for i in range(steps):
        write(i).wait()


def on_device(panel_col, look_cols, sketch_map, upper_inv, lower_inv, pivots):
    rows, width = look_cols.shape
    panel_t = panel_col.T
    piv_row = pivots.reshape(1, NB)
    vmem = pl.BlockSpec(memory_space=pltpu.VMEM)
    hbm = pl.BlockSpec(memory_space=pltpu.HBM)
    inputs = [
        pltpu.with_memory_space_constraint(a, pltpu.HBM)
        for a in (pivots, piv_row, panel_t, look_cols, sketch_map, upper_inv, lower_inv)
    ]
    results = pl.pallas_call(
        exchange_kernel,
        out_shape=(
            jax.ShapeDtypeStruct((rows, 3 * NB), BF16),
            jax.ShapeDtypeStruct((3 * NB, width), BF16),
            jax.ShapeDtypeStruct((2 * NB, width), BF16),
            jax.ShapeDtypeStruct((NB, width), F32),
            jax.ShapeDtypeStruct((64, rows), F32),
            jax.ShapeDtypeStruct((64, NB), F32),
        ),
        in_specs=[hbm] * len(inputs),
        out_specs=(vmem,) * 6,
        scratch_shapes=[
            pltpu.SMEM((NB,), jnp.int32),
            pltpu.VMEM((1, NB), jnp.int32),
            pltpu.VMEM((rows, 256), F32),
            pltpu.VMEM((rows, 256), F32),
            pltpu.VMEM((NB, rows), F32),
            pltpu.VMEM((NB, NB), F32),
            pltpu.VMEM((NB, NB), F32),
            pltpu.VMEM((NB, rows), F32),
            pltpu.VMEM((NB, rows), BF16),
            pltpu.VMEM((8, rows), F32),
            pltpu.VMEM((2, NB, 256), F32),
            pltpu.VMEM((NB, 256), F32),
            pltpu.VMEM((NB, 256), F32),
            pltpu.VMEM((3, 64, 256), F32),
            pltpu.VMEM((64, 256), F32),
            pltpu.VMEM((7, 8, 256), F32),
            pltpu.VMEM((NB, width), F32),
            pltpu.VMEM((NB, width), F32),
            pltpu.VMEM((NB, NB), F32),
            pltpu.VMEM((NB, NB), F32),
            pltpu.VMEM((128, NB), F32),
            pltpu.VMEM((64, NB), F32),
            pltpu.VMEM((64, NB), F32),
            pltpu.VMEM((3, 16, NB), F32),
            pltpu.VMEM((CZ, 16, NB), F32),
            pltpu.VMEM((128, NB), F32),
            pltpu.VMEM((NB, NB), BF16),
            pltpu.VMEM((NB, NB), BF16),
            pltpu.VMEM((NB, NB), BF16),
            pltpu.VMEM((NB, NB), BF16),
            pltpu.VMEM((128, NB), BF16),
            pltpu.SemaphoreType.DMA((9,)),
            pltpu.SemaphoreType.DMA((N_SEM,)),
            pltpu.SemaphoreType.DMA((N_SEM,)),
        ],
        compiler_params=pltpu.CompilerParams(
            collective_id=0, has_side_effects=True, vmem_limit_bytes=36 << 20
        ),
        name="exchange",
    )(*inputs)

    first = (lax.axis_index("row") * rows).astype(jnp.int32).reshape(1)
    tile = 256
    updated, lp, sk = pl.pallas_call(
        update_kernel,
        out_shape=(
            jax.ShapeDtypeStruct((rows, width), F32),
            jax.ShapeDtypeStruct((64, rows), F32),
            jax.ShapeDtypeStruct((64, NB), F32),
        ),
        in_specs=[pl.BlockSpec(memory_space=pltpu.SMEM)] + [vmem] * 7,
        out_specs=(hbm,) * 3,
        scratch_shapes=[
            pltpu.VMEM((rows // tile, tile, width), F32),
            pltpu.SemaphoreType.DMA((rows // tile,)),
            pltpu.SemaphoreType.DMA((2,)),
        ],
        compiler_params=pltpu.CompilerParams(vmem_limit_bytes=32 << 20),
        name="update",
    )(first, look_cols, *results)
    return lp.T, updated, sk.T


def solution(mesh):
    placed = (P("row", "col"), P("row", "col"), P(None, "row"), P(), P(), P())
    return jax.shard_map(
        on_device,
        mesh=mesh,
        in_specs=placed,
        out_specs=(P("row", "col"), P("row", "col"), P(None, "col")),
        check_vma=False,
    )
```
